256 devices in a mesh: dp: 8 (over y, core), fsdp: 32 (over x, z).
Axes of the slice: x: 4, y: 4, z: 8, core: 2. Of those that a mesh axis runs over, the one named last changes fastest.
Arguments:
- grad_parts: bfloat16 [8, 256, 512, 512], P('dp', None, 'fsdp'), may hold values from -6 to 6
- first_moment: bfloat16 [256, 512, 512], P('dp', 'fsdp'), may hold values from -4 to 4
- second_moment: float32 [256, 512, 512], P('dp', 'fsdp'), may hold values from 0.25 to 4
- left_basis: bfloat16 [8, 32, 2, 512, 512], P('dp', 'fsdp'), may hold values from -0.25 to 0.25
- right_basis: bfloat16 [8, 32, 2, 512, 512], P('dp', 'fsdp'), may hold values from -0.25 to 0.25
- owner_list: int32 [8, 32, 1], P('dp'), may hold values from 0 to 31; in each aligned block of 32 rows (0 to 31, 32 to 63, ..., all dimensions but the last counted through in order) at most 2 rows name the same one
Outputs:
- first_moment_new: bfloat16 [256, 512, 512], P('dp', 'fsdp')
- second_moment_new: float32 [256, 512, 512], P('dp', 'fsdp')
- update: bfloat16 [256, 512, 512], P('dp', 'fsdp')
The draws below stay inside these ranges and needn't reach their ends.
Inputs may be any that keep to these rules, and one draw needn't show every extreme that they name: `owner_list`: in each data group no owner holds more than 2 blocks, and some owner holds exactly 2.
All inputs are finite; a program needn't handle non-finite values.
Results may differ from the reference program's by a relative error of at most 0.022.
Values may be sent and summed in bfloat16 or wider, within the bound.
A program may use at most 64 MiB of HBM per device.

```python
import math
import jax
import jax.numpy as jnp
import numpy as np
from jax import lax

BLOCK = 512
GROUP_BLOCKS = 32
ALL_BLOCKS = 256
CAP = 2
N_DP = 8
N_FSDP = 32


def raised(result, own_key, source, target, shards_of, factor):
    owner, partner = [(jnp.arange(result.shape[dim]) // (result.shape[dim] // shards_of)).reshape([-1 if axis == dim else 1 for axis in range(result.ndim)]) for dim in (source, target)]
    chosen = jax.random.permutation(own_key, shards_of)[partner]
    strong = (owner == chosen) | (owner == (partner + shards_of // 2) % shards_of)
    return jnp.where(strong, factor * result, result)


def block_levels(key, extent, cuts, smallest, largest):
    gain = 1.0
    for dim, blocks in cuts:
        steps = jax.random.uniform(jax.random.fold_in(jax.random.fold_in(key, 6), dim), (blocks,), jnp.float32, smallest / len(cuts), largest / len(cuts))
        gain = gain * jnp.repeat(jnp.exp(steps), extent[dim] // blocks).reshape((-1,) + (1,) * (len(extent) - 1 - dim))
    return gain


def deal_out(rng, own, number, rows, number_of, top, limit, skew):
    sequence = jax.random.permutation(rng, number_of)
    crowded, usual = shares(number_of, rows * top, limit, skew, True), shares(number_of, rows * top, limit, skew, False)
    places = jnp.arange(number_of)

    def named(tallies, rotation):
        used = int((tallies > 0).sum())
        fixed = max(1, used // 4)
        shifted = fixed + (places - fixed + rotation * (used - fixed)) % max(1, number_of - fixed)
        return jnp.zeros((number_of,), jnp.int32).at[sequence[jnp.where(places < fixed, places, shifted)]].set(jnp.asarray(tallies, jnp.int32))

    tallies = jnp.where(number % 4 == 0, named(crowded, number // 4), named(usual, number - number // 4 - 1))
    mixed = jax.random.permutation(jax.random.fold_in(own, 3), number_of)
    donor, receiver = mixed[0:number_of // 2 * 2:2], mixed[1:number_of // 2 * 2:2]
    margin = jnp.minimum(tallies[donor] - 1, limit - tallies[receiver]) // 2
    margin = jnp.where((donor == sequence[0]) | (receiver == sequence[0]) | (tallies[receiver] == 0), 0, jnp.maximum(margin, 0))
    shifted = jax.random.randint(jax.random.fold_in(own, 4), (number_of // 2,), 0, 1 << 20) % (margin + 1)
    tallies = tallies.at[donor].add(-shifted).at[receiver].add(shifted)
    members = jnp.searchsorted(jnp.cumsum(tallies), jnp.arange(rows * top), side="right").astype(jnp.int32)
    table = members.reshape(top, rows).T
    table = table[jax.random.permutation(jax.random.fold_in(own, 1), rows)]
    rotation = jax.random.randint(jax.random.fold_in(own, 2), (rows, 1), 0, top)
    return jnp.take_along_axis(table, (jnp.arange(top)[None, :] + rotation) % top, axis=1)


def shares(amount, total, most, lean, full):
    weights = [(1 << 20) // math.isqrt(grade ** lean) + 1 for grade in range(1, amount + 1)]
    largest = most if full else min(most, max(-(-total // amount), total * weights[0] // sum(weights)))
    least = 1 if total - largest >= amount - 1 else 0
    holding, surplus = [largest] + [least] * (amount - 1), total - largest - least * (amount - 1)
    while surplus > 0:
        free = [i for i in range(1, amount) if holding[i] < largest] or [i for i in range(1, amount) if holding[i] < most]
        whole, left = sum([weights[i] for i in free]), surplus
        for i in free:
            extra = min(most - holding[i], max(1, left * weights[i] // whole), surplus)
            holding[i] = holding[i] + extra
            surplus = surplus - extra
    return np.array(holding)


def normal_values(key, extent, deviation, limit, cuts=(), kind=jnp.bfloat16):
    factor_of = block_levels(key, extent, cuts, -0.22, 0.18) if cuts else 1.0
    drawn = jax.random.normal(key, extent, jnp.float32) * deviation * factor_of
    return jnp.minimum(jnp.maximum(drawn, -limit), limit).astype(kind)


def bell_draw_with(rng, extent, spread, bound, split, heavy, held_as=jnp.bfloat16):
    drawn = spread * jax.random.normal(rng, extent, jnp.float32)
    if split:
        drawn = drawn * block_levels(rng, extent, split, -0.22, 0.18)
    return jnp.clip(raised(drawn, jax.random.fold_in(rng, 3), *heavy), -bound, bound).astype(held_as)


def setup_inputs(seed: int = 0) -> dict:
    seeds = jax.random.split(jax.random.key(seed), 7)
    grad_parts = bell_draw_with(seeds[0], (N_DP, ALL_BLOCKS, BLOCK, BLOCK), 1.0, 6.0, ((0, 8), (2, 32)), (0, 1, 8, 2.0))
    first_moment = normal_values(seeds[1], (ALL_BLOCKS, BLOCK, BLOCK), 0.5, 4.0, ((0, 8), (1, 32)))
    second_moment = jnp.clip(jnp.exp(math.log(4.0) - 2.7725887 * jax.random.uniform(seeds[2], (ALL_BLOCKS, BLOCK, BLOCK), jnp.float32) ** block_levels(seeds[2], (ALL_BLOCKS, BLOCK, BLOCK), ((0, 8), (1, 32)), -0.2, 0.2)), 0.25, 4.0)
    left_basis = normal_values(seeds[3], (N_DP, N_FSDP, CAP, BLOCK, BLOCK), BLOCK ** -0.5, 0.25, ((0, 8), (1, 32)))
    right_basis = normal_values(seeds[4], (N_DP, N_FSDP, CAP, BLOCK, BLOCK), BLOCK ** -0.5, 0.25, ((0, 8), (1, 32)))
    owner_list_keys = jax.random.split(jax.random.fold_in(seeds[5], 1), N_DP * GROUP_BLOCKS // GROUP_BLOCKS)
    owner_list_turns = jax.random.permutation(jax.random.fold_in(seeds[5], 3), N_DP * GROUP_BLOCKS // GROUP_BLOCKS)
    owner_list = jax.vmap(lambda own, number: deal_out(jax.random.fold_in(seeds[5], 2), own, number, GROUP_BLOCKS, N_FSDP, 1, CAP, 2))(owner_list_keys, owner_list_turns).reshape((N_DP, GROUP_BLOCKS, 1))
    return {"grad_parts": grad_parts, "first_moment": first_moment, "second_moment": second_moment, "left_basis": left_basis, "right_basis": right_basis, "owner_list": owner_list}


BETA_FIRST = 0.9
BETA_SECOND = 0.95
EPSILON = 1e-08

def slot_numbers(owners):
    how_many = owners.shape[0]
    ordinal = jnp.arange(how_many, dtype=jnp.int32)
    matching = owners[:, None] == owners[None, :]
    earlier = ordinal[None, :] < ordinal[:, None]
    return lax.optimization_barrier(jnp.sum(jnp.logical_and(matching, earlier).astype(jnp.int32), axis=1))

def rotate_block(gradient, moment_one, moment_two, left_side, right_side):
    half_rot = jnp.dot(gradient, right_side, preferred_element_type=jnp.float32).astype(jnp.bfloat16)
    rotated = jnp.dot(left_side.T, half_rot, preferred_element_type=jnp.float32).astype(jnp.bfloat16)
    rotated_wide = rotated.astype(jnp.float32)
    first_wide = BETA_FIRST * moment_one.astype(jnp.float32) + (1.0 - BETA_FIRST) * rotated_wide
    second_new = BETA_SECOND * moment_two + (1.0 - BETA_SECOND) * rotated_wide * rotated_wide
    direction = (first_wide / (jnp.sqrt(second_new) + EPSILON)).astype(jnp.bfloat16)
    back_half = jnp.dot(direction, right_side.T, preferred_element_type=jnp.float32).astype(jnp.bfloat16)
    update = jnp.dot(left_side, back_half, preferred_element_type=jnp.float32).astype(jnp.bfloat16)
    return (first_wide.astype(jnp.bfloat16), second_new, update)

def reference(grad_parts, first_moment, second_moment, left_basis, right_basis, owner_list):
    summed = jnp.zeros(grad_parts.shape[1:], jnp.float32)
    for data_group in range(N_DP):
        summed = summed + grad_parts[data_group].astype(jnp.float32)
    gradient = summed.astype(jnp.bfloat16)
    slot_table = jax.vmap(slot_numbers)(owner_list[:, :, 0])

    def per_block(position):
        group_id = position // GROUP_BLOCKS
        within = position % GROUP_BLOCKS
        owner_id = owner_list[group_id, within, 0]
        slot_here = slot_table[group_id, within]
        left_side = left_basis[group_id, owner_id, slot_here]
        right_side = right_basis[group_id, owner_id, slot_here]
        return rotate_block(gradient[position], first_moment[position], second_moment[position], left_side, right_side)
    first_new, second_new, update = lax.map(per_block, jnp.arange(ALL_BLOCKS, dtype=jnp.int32))
    return (first_new, second_new, update)
```

```python
import functools

import jax
import jax.numpy as jnp
from jax import lax
from jax.experimental import pallas as pl
from jax.experimental.pallas import tpu as pltpu
from jax.sharding import PartitionSpec as P

BETA_FIRST = 0.9
BETA_SECOND = 0.95
EPSILON = 1e-08

MESH = pl.DeviceIdType.MESH
NY = 4
CUTS = 2
SLOTS = 2


def z_order(nz):
    order = [0]
    for step in range(1, nz // 2 + 1):
        order.append(step)
        if nz - step != step:
            order.append(nz - step)
    return order


def adam(rotated, first, second):
    wide = rotated.astype(jnp.float32)
    first_wide = BETA_FIRST * first.astype(jnp.float32) + (1.0 - BETA_FIRST) * wide
    second_new = BETA_SECOND * second + (1.0 - BETA_SECOND) * wide * wide
    return first_wide, second_new


def kernel(
    nx, nz,
    src, tgt, grads, first_hbm, second_hbm, left_hbm, right_hbm,
    first_out, second_out, update_out,
    own, other, far_up, far_down, from_down, from_up, grad,
    g_send, g_recv, r_send, r_recv, d_send, d_recv, u_send, u_recv,
    first, second, left, right, left_t, total, half, back, first_new, second_new, update,
    load_sem, own_sem, pair_send, pair_recv, y_send, y_recv,
    g_ssem, g_rsem, r_ssem, r_rsem, d_ssem, d_rsem, u_ssem, u_rsem, out_sem,
):
    nf = nx * nz
    nb, rows, columns = first.shape
    width = columns // CUTS
    d, me = lax.axis_index("dp"), lax.axis_index("fsdp")
    y, core = d // 2, d % 2
    x, z = me // nz, me % nz
    up, down = (y + 1) % NY, (y + NY - 1) % NY
    at_up, at_down, at_pair = (up * 2 + core, me), (down * 2 + core, me), (y * 2 + 1 - core, me)
    order = z_order(nz)

    chips = [(y + 2) % NY, up, down, y]
    loads = [
        pltpu.make_async_copy(ref, to, load_sem.at[i])
        for i, (ref, to) in enumerate(
            [(left_hbm, left), (right_hbm, right), (first_hbm, first), (second_hbm, second)]
        )
    ]
    cols = [pl.ds(c * width, width) for c in range(CUTS)]
    owns = [
        [
            pltpu.make_async_copy(grads.at[chips[r], core, :, :, cols[c]], own.at[c, r], own_sem.at[c, r])
            for r in range(NY)
        ]
        for c in range(CUTS)
    ]
    for c in range(CUTS):
        for r in range(NY):
            owns[c][r].start()
    for load in loads:
        load.start()

    barrier = pltpu.get_barrier_semaphore()

    def greet(i, carry):
        for dz in order:
            p = ((x + i) % nx) * nz + (z + dz) % nz
            if dz == 0:
                @pl.when(i > 0)
                def _():
                    pl.semaphore_signal(barrier, inc=1, device_id=(d, p), device_id_type=MESH)
            else:
                pl.semaphore_signal(barrier, inc=1, device_id=(d, p), device_id_type=MESH)
        return carry

    for device in (at_pair, at_up, at_down):
        pl.semaphore_signal(barrier, inc=1, device_id=device, device_id_type=MESH)
    lax.fori_loop(0, nx, greet, 0)
    pl.semaphore_wait(barrier, nf - 1 + 3)

    def remote(source, target, send, recv, device):
        return pltpu.make_async_remote_copy(
            src_ref=source, dst_ref=target, send_sem=send, recv_sem=recv, device_id=device, device_id_type=MESH
        )

    pairs = [
        [
            remote(
                grads.at[chips[r], 1 - core, :, :, cols[c]], other.at[c, r],
                pair_send.at[c, r], pair_recv.at[c, r], at_pair,
            )
            for r in range(NY)
        ]
        for c in range(CUTS)
    ]
    for c in range(CUTS):
        for r in range(NY):
            pairs[c][r].start()

    low, high = pl.ds(0, nb // 2), pl.ds(nb // 2, nb // 2)
    hops = [
        [
            remote(own.at[c, 0, low], far_up.at[c], y_send.at[c, 0], y_recv.at[c, 0], at_up),
            remote(own.at[c, 0, high], far_down.at[c], y_send.at[c, 1], y_recv.at[c, 1], at_down),
            remote(own.at[c, 1, high], from_down.at[c, high], y_send.at[c, 2], y_recv.at[c, 2], at_up),
            remote(own.at[c, 2, low], from_up.at[c, low], y_send.at[c, 3], y_recv.at[c, 3], at_down),
            remote(own.at[c, 1, low], from_down.at[c, low], y_send.at[c, 4], y_recv.at[c, 4], at_up),
            remote(own.at[c, 2, high], from_up.at[c, high], y_send.at[c, 5], y_recv.at[c, 5], at_down),
        ]
        for c in range(CUTS)
    ]
    group = min(4, nb // 2)

    def wide(ref, *at):
        return ref[at].astype(jnp.float32)

    def pair_sum(c, r):
        owns[c][r].wait()
        pairs[c][r].wait_recv()

        def step(j, carry):
            blocks = pl.ds(j * group, group)
            own[c, r, blocks] = (wide(own, c, r, blocks) + wide(other, c, r, blocks)).astype(jnp.bfloat16)
            return carry

        lax.fori_loop(0, nb // group, step, 0)

    def add_far(c, r, far, first_block):
        def step(j, carry):
            blocks = pl.ds(first_block + j * group, group)
            own[c, r, blocks] = (wide(own, c, r, blocks) + wide(far, c, pl.ds(j * group, group))).astype(jnp.bfloat16)
            return carry

        lax.fori_loop(0, nb // 2 // group, step, 0)

    def spread(c):
        pair_sum(c, 0)
        hops[c][0].start()
        hops[c][1].start()
        pair_sum(c, 1)
        hops[c][2].start()
        pair_sum(c, 2)
        hops[c][3].start()

    def forward(c):
        hops[c][0].wait_recv()
        add_far(c, 1, far_up, 0)
        hops[c][4].start()
        hops[c][1].wait_recv()
        add_far(c, 2, far_down, nb // 2)
        hops[c][5].start()

    def finish(c):
        pair_sum(c, 3)
        for i in (2, 3, 4, 5):
            hops[c][i].wait_recv()

        def step(j, carry):
            blocks = pl.ds(j * group, group)
            grad[c, blocks] = (
                wide(own, c, 3, blocks) + wide(from_down, c, blocks) + wide(from_up, c, blocks)
            ).astype(jnp.bfloat16)
            return carry

        lax.fori_loop(0, nb // group, step, 0)

    def exchange(send, recv, at, ssem, rsem, fill_plane=None, fill=None):
        def plane(i, carry):
            px = (x + i) % nx
            if fill_plane is not None:
                fill_plane(px)
            for dz in order:
                p = px * nz + (z + dz) % nz
                if fill is not None:
                    fill(p)
                source, target = send.at[(*at, p)], recv.at[(*at, me)]
                if dz == 0:
                    @pl.when(i > 0)
                    def _():
                        remote(source, target, ssem, rsem, (d, p)).start()

                    @pl.when(i == 0)
                    def _():
                        recv[(*at, me)] = send[(*at, me)]
                else:
                    remote(source, target, ssem, rsem, (d, p)).start()
            return carry

        lax.fori_loop(0, nx, plane, 0)

    def arrived(ref, at, rsem):
        whole = ref.at[(*at, pl.ds(0, nf - 1))]
        pltpu.make_async_copy(whole, whole, rsem).wait()

    def send_grad(c, s):
        def fill(p):
            g_send[c, s, p] = grad_cut[c][src[s * nf + p]]

        exchange(g_send, g_recv, (c, s), g_ssem.at[c, s], g_rsem.at[c, s], fill=fill)

    grad_cut = [grad.at[c] for c in range(CUTS)]

    spread(0)
    forward(0)
    spread(1)
    for load in loads:
        load.wait()
    for s in range(SLOTS):
        for t in range(nx):
            piece = pl.ds(t * nz * rows, nz * rows)
            left_t[s, :, piece] = left[s, piece, :].T
    finish(0)
    for s in range(SLOTS):
        send_grad(0, s)
    forward(1)
    finish(1)
    for s in range(SLOTS):
        send_grad(1, s)

    span = nz * rows

    def product(c, s, t):
        held = g_recv[c, s, pl.ds(t * nz, nz)].reshape(span, width)
        return jnp.dot(held, right[s, cols[c], :], preferred_element_type=jnp.float32)

    for s in range(SLOTS):
        arrived(g_recv, (0, s), g_rsem.at[0, s])

        def first_half(t, carry, s=s):
            total[s, pl.ds(t * span, span)] = product(0, s, t)
            return carry

        lax.fori_loop(0, nx, first_half, 0)

    for s in range(SLOTS):
        arrived(g_recv, (1, s), g_rsem.at[1, s])

        def second_half(t, carry, s=s):
            piece = pl.ds(t * span, span)
            half[s, piece] = (total[s, piece] + product(1, s, t)).astype(jnp.bfloat16)
            return carry

        lax.fori_loop(0, nx, second_half, 0)

        def rotate(px, s=s):
            made = jnp.dot(left_t[s, pl.ds(px * span, span)], half[s], preferred_element_type=jnp.float32)
            r_send[s, pl.ds(px * nz, nz)] = made.astype(jnp.bfloat16).reshape(nz, rows, columns)

        exchange(r_send, r_recv, (s,), r_ssem.at[s], r_rsem.at[s], fill_plane=rotate)

    for s in range(SLOTS):
        arrived(r_recv, (s,), r_rsem.at[s])

        def direct(p, s=s):
            block = src[s * nf + p]
            first_wide, second_wide = adam(r_recv[s, p], first[block], second[block])
            d_send[s, p] = (first_wide / (jnp.sqrt(second_wide) + EPSILON)).astype(jnp.bfloat16)

        exchange(d_send, d_recv, (s,), d_ssem.at[s], d_rsem.at[s], fill=direct)

    def moments(j, carry):
        first_wide, second_wide = adam(r_recv[tgt[j] // nf, tgt[j] % nf], first[j], second[j])
        first_new[j] = first_wide.astype(jnp.bfloat16)
        second_new[j] = second_wide
        return carry

    lax.fori_loop(0, nb, moments, 0)
    outs = [
        pltpu.make_async_copy(ref, to, out_sem.at[i])
        for i, (ref, to) in enumerate([(first_new, first_out), (second_new, second_out), (update, update_out)])
    ]
    outs[0].start()
    outs[1].start()

    for s in range(SLOTS):
        arrived(d_recv, (s,), d_rsem.at[s])

        def undo_right(t, carry, s=s):
            held = d_recv[s, pl.ds(t * nz, nz)].reshape(span, columns)
            made = lax.dot_general(held, right[s], (((1,), (1,)), ((), ())), preferred_element_type=jnp.float32)
            back[s, pl.ds(t * span, span)] = made.astype(jnp.bfloat16)
            return carry

        lax.fori_loop(0, nx, undo_right, 0)

        def undo_left(px, s=s):
            made = jnp.dot(left[s, pl.ds(px * span, span)], back[s], preferred_element_type=jnp.float32)
            u_send[s, pl.ds(px * nz, nz)] = made.astype(jnp.bfloat16).reshape(nz, rows, columns)

        exchange(u_send, u_recv, (s,), u_ssem.at[s], u_rsem.at[s], fill_plane=undo_left)

    for s in range(SLOTS):
        arrived(u_recv, (s,), u_rsem.at[s])

    def pick(j, carry):
        update[j] = u_recv[tgt[j] // nf, tgt[j] % nf]
        return carry

    lax.fori_loop(0, nb, pick, 0)
    outs[2].start()

    for c in range(CUTS):
        for r in range(NY):
            pairs[c][r].wait_send()
        for hop in hops[c]:
            hop.wait_send()
        for s in range(SLOTS):
            arrived(g_send, (c, s), g_ssem.at[c, s])
    for s in range(SLOTS):
        arrived(r_send, (s,), r_ssem.at[s])
        arrived(d_send, (s,), d_ssem.at[s])
        arrived(u_send, (s,), u_ssem.at[s])
    for out in outs:
        out.wait()


def tables(owners, nf):
    nb = owners.shape[0]
    ordinal = jnp.arange(nb, dtype=jnp.int32)
    matching = owners[:, None] == owners[None, :]
    earlier = ordinal[None, :] < ordinal[:, None]
    slot = jnp.sum(jnp.logical_and(matching, earlier).astype(jnp.int32), axis=1)
    target = slot * nf + owners
    picked = jnp.arange(SLOTS * nf, dtype=jnp.int32)[:, None] == target[None, :]
    source = jnp.sum(jnp.where(picked, ordinal[None, :], 0), axis=1)
    return source, target


def per_device(nx, nz, grad_parts, first_moment, second_moment, left_basis, right_basis, owner_list):
    nf = nx * nz
    nb, rows, columns = first_moment.shape
    width = columns // CUTS
    source, target = tables(owner_list[0, :, 0], nf)
    grads = grad_parts.reshape(NY, 2, nb, rows, columns)
    bf16, f32 = jnp.bfloat16, jnp.float32
    dma = pltpu.SemaphoreType.DMA
    order = nf * rows
    moved = pltpu.VMEM((SLOTS, nf, rows, columns), bf16)
    cut = pltpu.VMEM((CUTS, SLOTS, nf, rows, width), bf16)
    square = pltpu.VMEM((SLOTS, order, columns), bf16)
    hbm = pl.BlockSpec(memory_space=pl.ANY)
    smem = pl.BlockSpec(memory_space=pltpu.SMEM)
    return pl.pallas_call(
        functools.partial(kernel, nx, nz),
        out_shape=(
            jax.ShapeDtypeStruct((nb, rows, columns), bf16),
            jax.ShapeDtypeStruct((nb, rows, columns), f32),
            jax.ShapeDtypeStruct((nb, rows, columns), bf16),
        ),
        in_specs=[smem, smem, hbm, hbm, hbm, hbm, hbm],
        out_specs=(hbm, hbm, hbm),
        scratch_shapes=[
            pltpu.VMEM((CUTS, NY, nb, rows, width), bf16),
            pltpu.VMEM((CUTS, NY, nb, rows, width), bf16),
            pltpu.VMEM((CUTS, nb // 2, rows, width), bf16),
            pltpu.VMEM((CUTS, nb // 2, rows, width), bf16),
            pltpu.VMEM((CUTS, nb, rows, width), bf16),
            pltpu.VMEM((CUTS, nb, rows, width), bf16),
            pltpu.VMEM((CUTS, nb, rows, width), bf16),
            cut, cut, moved, moved, moved, moved, moved, moved,
            pltpu.VMEM((nb, rows, columns), bf16),
            pltpu.VMEM((nb, rows, columns), f32),
            square, square, square,
            pltpu.VMEM((SLOTS, order, columns), f32),
            square, square,
            pltpu.VMEM((nb, rows, columns), bf16),
            pltpu.VMEM((nb, rows, columns), f32),
            pltpu.VMEM((nb, rows, columns), bf16),
            dma((4,)), dma((CUTS, NY)), dma((CUTS, NY)), dma((CUTS, NY)), dma((CUTS, 6)), dma((CUTS, 6)),
            dma((CUTS, SLOTS)), dma((CUTS, SLOTS)),
            dma((SLOTS,)), dma((SLOTS,)), dma((SLOTS,)), dma((SLOTS,)), dma((SLOTS,)), dma((SLOTS,)),
            dma((3,)),
        ],
        compiler_params=pltpu.CompilerParams(
            collective_id=0, has_side_effects=True, vmem_limit_bytes=48 * 1024 * 1024
        ),
        cost_estimate=pl.CostEstimate(
            flops=SLOTS * 8 * order * columns * columns, bytes_accessed=16 * 1024 * 1024, transcendentals=0
        ),
    )(source, target, grads, first_moment, second_moment, left_basis[0, 0], right_basis[0, 0])


def solution(mesh):
    nf = mesh.shape["fsdp"]
    nz = min(8, nf // 2)
    placed = (
        P("dp", None, "fsdp", None),
        P("dp", "fsdp", None),
        P("dp", "fsdp", None),
        P("dp", "fsdp", None, None, None),
        P("dp", "fsdp", None, None, None),
        P("dp", None, None),
    )
    return jax.shard_map(
        functools.partial(per_device, nf // nz, nz),
        mesh=mesh,
        in_specs=placed,
        out_specs=(P("dp", "fsdp", None), P("dp", "fsdp", None), P("dp", "fsdp", None)),
        check_vma=False,
    )
```

```python
import functools

import jax
import jax.numpy as jnp
from jax import lax
from jax.experimental import pallas as pl
from jax.experimental.pallas import tpu as pltpu
from jax.sharding import PartitionSpec as P

BETA_FIRST = 0.9
BETA_SECOND = 0.95
EPSILON = 1e-08

MESH = pl.DeviceIdType.MESH
VMEM_BYTES = 60 * 1024 * 1024
NY = 4
SLOTS = 2
CUTS = ((2, True, True), (2, False, True), (4, False, False))
NC = len(CUTS)


def column_cuts(columns):
    widths = [columns * eighths // 8 for eighths, _, _ in CUTS]
    return [sum(widths[:c]) for c in range(NC)], widths


def z_order(nz):
    order = [0]
    for step in range(1, nz // 2 + 1):
        order.append(step)
        if nz - step != step:
            order.append(nz - step)
    return order


def adam(rotated, first, second):
    wide = rotated.astype(jnp.float32)
    first_wide = BETA_FIRST * first.astype(jnp.float32) + (1.0 - BETA_FIRST) * wide
    second_new = BETA_SECOND * second + (1.0 - BETA_SECOND) * wide * wide
    return first_wide, second_new


def kernel(
    nx, nz,
    owners, grads, first_hbm, second_hbm, left_hbm, right_hbm,
    first_out, second_out, update_out,
    *scratch,
):
    cut_refs = [scratch[c * 8:c * 8 + 8] for c in range(NC)]
    own, other, far, from_down, from_up, grad, g_send, g_recv = zip(*cut_refs)
    (
        table, places,
        r_send, r_recv, d_send, d_recv, u_send, u_recv,
        first, second, left, right, left_t, total, half, back, first_new, second_new, update,
        load_sem, own_sem, pair_send, pair_recv, y_send, y_recv,
        g_ssem, g_rsem, r_ssem, r_rsem, d_ssem, d_rsem, u_ssem, u_rsem, out_sem,
    ) = scratch[NC * 8:]
    nf = nx * nz
    nb, rows, columns = first.shape
    starts, widths = column_cuts(columns)
    d, me = lax.axis_index("dp"), lax.axis_index("fsdp")
    y, core = d // 2, d % 2
    x, z = me // nz, me % nz
    up, down = (y + 1) % NY, (y + NY - 1) % NY
    at_up, at_down, at_pair = (up * 2 + core, me), (down * 2 + core, me), (y * 2 + 1 - core, me)
    at_far = (((y + 2) % NY) * 2 + core, me)
    order = z_order(nz)

    chips = [(y + 2) % NY, up, down, y]
    loads = [
        pltpu.make_async_copy(ref, to, load_sem.at[i])
        for i, (ref, to) in enumerate(
            [(left_hbm, left), (right_hbm, right), (first_hbm, first), (second_hbm, second)]
        )
    ]
    cols = [pl.ds(starts[c], widths[c]) for c in range(NC)]
    owns = [
        [
            pltpu.make_async_copy(grads.at[chips[r], core, :, :, cols[c]], own[c].at[r], own_sem.at[c, r])
            for r in range(NY)
        ]
        for c in range(NC)
    ]
    for c in range(NC):
        for r in range(NY):
            owns[c][r].start()
    for load in loads:
        load.start()

    def find_places():
        lane = lax.broadcasted_iota(jnp.int32, (8, 128), 1)
        zero = jnp.zeros((8, 128), jnp.int32)

        def step(j, carry):
            count, source, named = carry
            owner = owners[j]
            match = lane % nf == owner
            source = jnp.where(jnp.logical_and(match, count == lane // nf), j, source)
            return count + match.astype(jnp.int32), source, jnp.where(lane == j, owner, named)

        _, source, named = lax.fori_loop(0, nb, step, (zero, zero, zero))

        def earlier(i, slot):
            return slot + jnp.logical_and(named == owners[i], lane > i).astype(jnp.int32)

        table[0:8] = source
        table[8:16] = jnp.minimum(lax.fori_loop(0, nb, earlier, zero), SLOTS - 1) * nf + named
        copy = pltpu.make_async_copy(table, places, load_sem.at[4])
        copy.start()
        copy.wait()

    barrier = pltpu.get_barrier_semaphore()

    def greet(i, carry):
        for dz in order:
            p = ((x + i) % nx) * nz + (z + dz) % nz
            if dz == 0:
                @pl.when(i > 0)
                def _():
                    pl.semaphore_signal(barrier, inc=1, device_id=(d, p), device_id_type=MESH)
            else:
                pl.semaphore_signal(barrier, inc=1, device_id=(d, p), device_id_type=MESH)
        return carry

    for device in (at_pair, at_far, at_up, at_down):
        pl.semaphore_signal(barrier, inc=1, device_id=device, device_id_type=MESH)
    lax.fori_loop(0, nx, greet, 0)
    pl.semaphore_wait(barrier, nf - 1 + 4)

    def remote(source, target, send, recv, device):
        return pltpu.make_async_remote_copy(
            src_ref=source, dst_ref=target, send_sem=send, recv_sem=recv, device_id=device, device_id_type=MESH
        )

    pairs = [
        [
            remote(
                grads.at[chips[r], 1 - core, :, :, cols[c]], other[c].at[r],
                pair_send.at[c, r], pair_recv.at[c, r], at_pair,
            )
            for r in range(NY)
        ]
        for c in range(NC)
    ]
    for c in range(NC):
        for r in range(NY):
            pairs[c][r].start()

    low, high = pl.ds(0, nb // 2), pl.ds(nb // 2, nb // 2)

    def y_hop(c, i, source, target, device):
        return remote(source, target, y_send.at[c, i], y_recv.at[c, i], device)

    hops = [
        [
            y_hop(c, 0, own[c].at[0], far[c], at_far),
            y_hop(c, 1, own[c].at[1], from_down[c], at_up),
            y_hop(c, 2, own[c].at[2], from_up[c], at_down),
        ]
        if CUTS[c][1]
        else [
            y_hop(c, 0, own[c].at[0, low], far[c].at[low], at_up),
            y_hop(c, 1, own[c].at[0, high], far[c].at[high], at_down),
            y_hop(c, 2, own[c].at[1, high], from_down[c].at[high], at_up),
            y_hop(c, 3, own[c].at[2, low], from_up[c].at[low], at_down),
            y_hop(c, 4, own[c].at[1, low], from_down[c].at[low], at_up),
            y_hop(c, 5, own[c].at[2, high], from_up[c].at[high], at_down),
        ]
        for c in range(NC)
    ]
    group = min(4, nb // 2)

    def wide(ref, *at):
        return ref[at].astype(jnp.float32)

    def pair_sum(c, r):
        owns[c][r].wait()
        pairs[c][r].wait_recv()

        def step(j, carry):
            blocks = pl.ds(j * group, group)
            own[c][r, blocks] = (wide(own[c], r, blocks) + wide(other[c], r, blocks)).astype(jnp.bfloat16)
            return carry

        lax.fori_loop(0, nb // group, step, 0)

    def add_far(c, r, first_block):
        def step(j, carry):
            blocks = pl.ds(first_block + j * group, group)
            own[c][r, blocks] = (wide(own[c], r, blocks) + wide(far[c], blocks)).astype(jnp.bfloat16)
            return carry

        lax.fori_loop(0, nb // 2 // group, step, 0)

    def spread(c):
        pair_sum(c, 0)
        hops[c][0].start()
        if not CUTS[c][1]:
            hops[c][1].start()
        pair_sum(c, 1)
        hops[c][1 if CUTS[c][1] else 2].start()
        pair_sum(c, 2)
        hops[c][2 if CUTS[c][1] else 3].start()

    def forward(c):
        if CUTS[c][1]:
            return
        hops[c][0].wait_recv()
        add_far(c, 1, 0)
        hops[c][4].start()
        hops[c][1].wait_recv()
        add_far(c, 2, nb // 2)
        hops[c][5].start()

    def finish(c):
        pair_sum(c, 3)
        straight = CUTS[c][1]
        for hop in hops[c][0 if straight else 2:]:
            hop.wait_recv()

        def step(j, carry):
            blocks = pl.ds(j * group, group)
            summed = wide(own[c], 3, blocks) + wide(from_down[c], blocks) + wide(from_up[c], blocks)
            if straight:
                summed = summed + wide(far[c], blocks)
            grad[c][blocks] = summed.astype(jnp.bfloat16)
            return carry

        lax.fori_loop(0, nb // group, step, 0)

    def exchange(send, recv, at, ssem, rsem, fill_plane=None, fill=None, flat=False):
        mine = (at[0] * nf + me,) if flat else (*at, me)

        def plane(i, carry):
            px = (x + i) % nx
            if fill_plane is not None:
                fill_plane(px)
            for dz in order:
                p = px * nz + (z + dz) % nz
                if fill is not None:
                    fill(p)
                source, target = send.at[(*at, p)], recv.at[mine]
                if dz == 0:
                    @pl.when(i > 0)
                    def _():
                        remote(source, target, ssem, rsem, (d, p)).start()

                    @pl.when(i == 0)
                    def _():
                        recv[mine] = send[(*at, me)]
                else:
                    remote(source, target, ssem, rsem, (d, p)).start()
            return carry

        lax.fori_loop(0, nx, plane, 0)

    def arrived(ref, at, rsem, flat=False):
        whole = ref.at[pl.ds(at[0] * nf, nf - 1)] if flat else ref.at[(*at, pl.ds(0, nf - 1))]
        pltpu.make_async_copy(whole, whole, rsem).wait()

    def send_grad(c, stream):
        per = SLOTS if CUTS[c][2] else 1

        def fill(p):
            for i in range(per):
                g_send[c][stream, p, i] = grad[c][places[0, (stream * per + i) * nf + p]]

        exchange(g_send[c], g_recv[c], (stream,), g_ssem.at[c, stream], g_rsem.at[c, stream], fill=fill)

    streams = [range(1) if CUTS[c][2] else range(SLOTS) for c in range(NC)]
    span = nz * rows

    def product(c, s, t):
        at = (0, pl.ds(t * nz, nz), s) if CUTS[c][2] else (s, pl.ds(t * nz, nz), 0)
        held = g_recv[c][at].reshape(span, widths[c])
        return jnp.dot(held, right[s, cols[c], :], preferred_element_type=jnp.float32)

    def add_products(c, s):
        def step(t, carry):
            piece = pl.ds(t * span, span)
            made = product(c, s, t)
            if c > 0:
                made = total[s, piece] + made
            if c < NC - 1:
                total[s, piece] = made
            else:
                half[s, piece] = made.astype(jnp.bfloat16)
            return carry

        lax.fori_loop(0, nx, step, 0)

    spread(0)
    for c in range(1, NC):
        spread(c)
        if c == 1:
            find_places()
        finish(c - 1)
        for stream in streams[c - 1]:
            send_grad(c - 1, stream)
        forward(c)
    for load in loads:
        load.wait()
    for s in range(SLOTS):
        for t in range(nx):
            piece = pl.ds(t * nz * rows, nz * rows)
            left_t[s, :, piece] = left[s, piece, :].T
    finish(NC - 1)
    for stream in streams[NC - 1]:
        send_grad(NC - 1, stream)

    for c in range(NC - 1):
        for stream in streams[c]:
            arrived(g_recv[c], (stream,), g_rsem.at[c, stream])
        for s in range(SLOTS):
            add_products(c, s)

    for s in range(SLOTS):
        if s < len(streams[NC - 1]):
            arrived(g_recv[NC - 1], (s,), g_rsem.at[NC - 1, s])
        add_products(NC - 1, s)

        def rotate(px, s=s):
            made = jnp.dot(left_t[s, pl.ds(px * span, span)], half[s], preferred_element_type=jnp.float32)
            r_send[s, pl.ds(px * nz, nz)] = made.astype(jnp.bfloat16).reshape(nz, rows, columns)

        exchange(r_send, r_recv, (s,), r_ssem.at[s], r_rsem.at[s], fill_plane=rotate, flat=True)

    for s in range(SLOTS):
        arrived(r_recv, (s,), r_rsem.at[s], flat=True)

        def direct(p, s=s):
            block = places[0, s * nf + p]
            first_wide, second_wide = adam(r_recv[s * nf + p], first[block], second[block])
            d_send[s, p] = (first_wide / (jnp.sqrt(second_wide) + EPSILON)).astype(jnp.bfloat16)

        exchange(d_send, d_recv, (s,), d_ssem.at[s], d_rsem.at[s], fill=direct)

    def moments(j, carry):
        first_wide, second_wide = adam(r_recv[places[8, j]], first[j], second[j])
        first_new[j] = first_wide.astype(jnp.bfloat16)
        second_new[j] = second_wide
        return carry

    lax.fori_loop(0, nb, moments, 0)
    outs = [
        pltpu.make_async_copy(ref, to, out_sem.at[i])
        for i, (ref, to) in enumerate([(first_new, first_out), (second_new, second_out), (update, update_out)])
    ]
    outs[0].start()
    outs[1].start()

    for s in range(SLOTS):
        arrived(d_recv, (s,), d_rsem.at[s])

        def undo_right(t, carry, s=s):
            held = d_recv[s, pl.ds(t * nz, nz)].reshape(span, columns)
            made = lax.dot_general(held, right[s], (((1,), (1,)), ((), ())), preferred_element_type=jnp.float32)
            back[s, pl.ds(t * span, span)] = made.astype(jnp.bfloat16)
            return carry

        lax.fori_loop(0, nx, undo_right, 0)

        def undo_left(px, s=s):
            made = jnp.dot(left[s, pl.ds(px * span, span)], back[s], preferred_element_type=jnp.float32)
            u_send[s, pl.ds(px * nz, nz)] = made.astype(jnp.bfloat16).reshape(nz, rows, columns)

        exchange(u_send, u_recv, (s,), u_ssem.at[s], u_rsem.at[s], fill_plane=undo_left, flat=True)

    for s in range(SLOTS):
        arrived(u_recv, (s,), u_rsem.at[s], flat=True)

    def pick(j, carry):
        update[j] = u_recv[places[8, j]]
        return carry

    lax.fori_loop(0, nb, pick, 0)
    outs[2].start()

    for c in range(NC):
        for r in range(NY):
            pairs[c][r].wait_send()
        for hop in hops[c]:
            hop.wait_send()
        for s in streams[c]:
            arrived(g_send[c], (s,), g_ssem.at[c, s])
    for s in range(SLOTS):
        arrived(r_send, (s,), r_ssem.at[s])
        arrived(d_send, (s,), d_ssem.at[s])
        arrived(u_send, (s,), u_ssem.at[s])
    for out in outs:
        out.wait()


def per_device(nx, nz, grad_parts, first_moment, second_moment, left_basis, right_basis, owner_list):
    nf = nx * nz
    nb, rows, columns = first_moment.shape
    grads = grad_parts.reshape(NY, 2, nb, rows, columns)
    bf16, f32 = jnp.bfloat16, jnp.float32
    dma = pltpu.SemaphoreType.DMA
    order = nf * rows
    moved = pltpu.VMEM((SLOTS, nf, rows, columns), bf16)
    flat = pltpu.VMEM((SLOTS * nf, rows, columns), bf16)
    square = pltpu.VMEM((SLOTS, order, columns), bf16)
    hbm = pl.BlockSpec(memory_space=pl.ANY)
    smem = pl.BlockSpec(memory_space=pltpu.SMEM)
    cut_scratch = []
    for (_, _, merged), width in zip(CUTS, column_cuts(columns)[1]):
        part = pltpu.VMEM((NY, nb, rows, width), bf16)
        group = pltpu.VMEM((nb, rows, width), bf16)
        per = SLOTS if merged else 1
        sent = pltpu.VMEM((SLOTS // per, nf, per, rows, width), bf16)
        cut_scratch += [part, part, group, group, group, group, sent, sent]
    return pl.pallas_call(
        functools.partial(kernel, nx, nz),
        out_shape=(
            jax.ShapeDtypeStruct((nb, rows, columns), bf16),
            jax.ShapeDtypeStruct((nb, rows, columns), f32),
            jax.ShapeDtypeStruct((nb, rows, columns), bf16),
        ),
        in_specs=[smem, hbm, hbm, hbm, hbm, hbm],
        out_specs=(hbm, hbm, hbm),
        scratch_shapes=cut_scratch + [
            pltpu.VMEM((16, 128), jnp.int32), pltpu.SMEM((16, 128), jnp.int32),
            moved, flat, moved, moved, moved, flat,
            pltpu.VMEM((nb, rows, columns), bf16),
            pltpu.VMEM((nb, rows, columns), f32),
            square, square, square,
            pltpu.VMEM((SLOTS, order, columns), f32),
            square, square,
            pltpu.VMEM((nb, rows, columns), bf16),
            pltpu.VMEM((nb, rows, columns), f32),
            pltpu.VMEM((nb, rows, columns), bf16),
            dma((5,)), dma((NC, NY)), dma((NC, NY)), dma((NC, NY)), dma((NC, 6)), dma((NC, 6)),
            dma((NC, SLOTS)), dma((NC, SLOTS)),
            dma((SLOTS,)), dma((SLOTS,)), dma((SLOTS,)), dma((SLOTS,)), dma((SLOTS,)), dma((SLOTS,)),
            dma((3,)),
        ],
        compiler_params=pltpu.CompilerParams(
            collective_id=0, has_side_effects=True, vmem_limit_bytes=VMEM_BYTES
        ),
        cost_estimate=pl.CostEstimate(
            flops=SLOTS * 8 * order * columns * columns, bytes_accessed=16 * 1024 * 1024, transcendentals=0
        ),
    )(
        owner_list.reshape(nb), grads, first_moment, second_moment,
        left_basis.reshape(SLOTS, order, order), right_basis.reshape(SLOTS, columns, columns),
    )


def solution(mesh):
    nf = mesh.shape["fsdp"]
    nz = min(8, nf // 2)
    placed = (
        P("dp", None, "fsdp", None),
        P("dp", "fsdp", None),
        P("dp", "fsdp", None),
        P("dp", "fsdp", None, None, None),
        P("dp", "fsdp", None, None, None),
        P("dp", None, None),
    )
    return jax.shard_map(
        functools.partial(per_device, nf // nz, nz),
        mesh=mesh,
        in_specs=placed,
        out_specs=(P("dp", "fsdp", None), P("dp", "fsdp", None), P("dp", "fsdp", None)),
        check_vma=False,
    )
```

```python
import functools

import jax
import jax.numpy as jnp
from jax import lax
from jax.experimental import pallas as pl
from jax.experimental.pallas import tpu as pltpu
from jax.sharding import PartitionSpec as P

BETA_FIRST = 0.9
BETA_SECOND = 0.95
EPSILON = 1e-08

MESH = pl.DeviceIdType.MESH
VMEM_BYTES = 32 * 1024 * 1024
NY = 4
SLOTS = 2
CUTS = ((2, True, True), (2, False, True), (2, False, True), (2, False, False))
NC = len(CUTS)


def column_cuts(columns):
    widths = [columns * eighths // 8 for eighths, _, _ in CUTS]
    return [sum(widths[:c]) for c in range(NC)], widths


def z_order(nz):
    order = [0]
    for step in range(1, nz // 2 + 1):
        order.append(step)
        if nz - step != step:
            order.append(nz - step)
    return order


def adam(rotated, first, second):
    wide = rotated.astype(jnp.float32)
    first_wide = BETA_FIRST * first.astype(jnp.float32) + (1.0 - BETA_FIRST) * wide
    second_new = BETA_SECOND * second + (1.0 - BETA_SECOND) * wide * wide
    return first_wide, second_new


def kernel(
    nx, nz,
    owners, grads, first_hbm, second_hbm, left_hbm, right_hbm,
    first_new, second_new, u_recv, table,
    *scratch,
):
    cut_refs = [scratch[c * 8:c * 8 + 8] for c in range(NC)]
    own, other, far, from_down, from_up, grad, g_send, g_recv = zip(*cut_refs)
    (
        places,
        r_send, r_recv, d_send, d_recv, u_send,
        first, second, left, right, left_t, total, half, back,
        load_sem, own_sem, pair_send, pair_recv, y_send, y_recv,
        g_ssem, g_rsem, r_ssem, r_rsem, d_ssem, d_rsem, u_ssem, u_rsem,
    ) = scratch[NC * 8:]
    nf = nx * nz
    nb, rows, columns = first.shape
    starts, widths = column_cuts(columns)
    d, me = lax.axis_index("dp"), lax.axis_index("fsdp")
    y, core = d // 2, d % 2
    x, z = me // nz, me % nz
    up, down = (y + 1) % NY, (y + NY - 1) % NY
    at_up, at_down, at_pair = (up * 2 + core, me), (down * 2 + core, me), (y * 2 + 1 - core, me)
    at_far = (((y + 2) % NY) * 2 + core, me)
    order = z_order(nz)

    chips = [(y + 2) % NY, up, down, y]
    loads = [
        pltpu.make_async_copy(ref, to, load_sem.at[i])
        for i, (ref, to) in enumerate(
            [(left_hbm, left), (right_hbm, right), (first_hbm, first), (second_hbm, second)]
        )
    ]
    cols = [pl.ds(starts[c], widths[c]) for c in range(NC)]
    owns = [
        [
            pltpu.make_async_copy(grads.at[chips[r], core, :, :, cols[c]], own[c].at[r], own_sem.at[c, r])
            for r in range(NY)
        ]
        for c in range(NC)
    ]
    for r in range(NY):
        owns[0][r].start()

    def find_places():
        lane = lax.broadcasted_iota(jnp.int32, (8, 128), 1)
        zero = jnp.zeros((8, 128), jnp.int32)

        def step(j, carry):
            count, source, named = carry
            owner = owners[j]
            match = lane % nf == owner
            source = jnp.where(jnp.logical_and(match, count == lane // nf), j, source)
            return count + match.astype(jnp.int32), source, jnp.where(lane == j, owner, named)

        _, source, named = lax.fori_loop(0, nb, step, (zero, zero, zero))

        def earlier(i, slot):
            return slot + jnp.logical_and(named == owners[i], lane > i).astype(jnp.int32)

        table[0:8] = source
        table[8:16] = jnp.minimum(lax.fori_loop(0, nb, earlier, zero), SLOTS - 1) * nf + named
        copy = pltpu.make_async_copy(table, places, load_sem.at[4])
        copy.start()
        copy.wait()

    barrier = pltpu.get_barrier_semaphore()

    def greet(i, carry):
        for dz in order:
            p = ((x + i) % nx) * nz + (z + dz) % nz
            if dz == 0:
                @pl.when(i > 0)
                def _():
                    pl.semaphore_signal(barrier, inc=1, device_id=(d, p), device_id_type=MESH)
            else:
                pl.semaphore_signal(barrier, inc=1, device_id=(d, p), device_id_type=MESH)
        return carry

    for device in (at_pair, at_far, at_up, at_down):
        pl.semaphore_signal(barrier, inc=1, device_id=device, device_id_type=MESH)
    lax.fori_loop(0, nx, greet, 0)
    pl.semaphore_wait(barrier, nf - 1 + 4)

    def remote(source, target, send, recv, device):
        return pltpu.make_async_remote_copy(
            src_ref=source, dst_ref=target, send_sem=send, recv_sem=recv, device_id=device, device_id_type=MESH
        )

    pairs = [
        [
            remote(
                grads.at[chips[r], 1 - core, :, :, cols[c]], other[c].at[r],
                pair_send.at[c, r], pair_recv.at[c, r], at_pair,
            )
            for r in range(NY)
        ]
        for c in range(NC)
    ]
    for c in range(NC):
        for r in range(NY):
            pairs[c][r].start()
            if c > 0:
                owns[c][r].start()
    for load in loads:
        load.start()

    low, high = pl.ds(0, nb // 2), pl.ds(nb // 2, nb // 2)

    def y_hop(c, i, source, target, device):
        return remote(source, target, y_send.at[c, i], y_recv.at[c, i], device)

    hops = [
        [
            y_hop(c, 0, own[c].at[0], far[c], at_far),
            y_hop(c, 1, own[c].at[1], from_down[c], at_up),
            y_hop(c, 2, own[c].at[2], from_up[c], at_down),
        ]
        if CUTS[c][1]
        else [
            y_hop(c, 0, own[c].at[0, low], far[c].at[low], at_up),
            y_hop(c, 1, own[c].at[0, high], far[c].at[high], at_down),
            y_hop(c, 2, own[c].at[1, high], from_down[c].at[high], at_up),
            y_hop(c, 3, own[c].at[2, low], from_up[c].at[low], at_down),
            y_hop(c, 4, own[c].at[1, low], from_down[c].at[low], at_up),
            y_hop(c, 5, own[c].at[2, high], from_up[c].at[high], at_down),
        ]
        for c in range(NC)
    ]
    group = min(4, nb // 2)

    def wide(ref, *at):
        return ref[at].astype(jnp.float32)

    def pair_sum(c, r):
        owns[c][r].wait()
        pairs[c][r].wait_recv()

        def step(j, carry):
            blocks = pl.ds(j * group, group)
            own[c][r, blocks] = (wide(own[c], r, blocks) + wide(other[c], r, blocks)).astype(jnp.bfloat16)
            return carry

        lax.fori_loop(0, nb // group, step, 0)

    def add_far(c, r, first_block):
        def step(j, carry):
            blocks = pl.ds(first_block + j * group, group)
            own[c][r, blocks] = (wide(own[c], r, blocks) + wide(far[c], blocks)).astype(jnp.bfloat16)
            return carry

        lax.fori_loop(0, nb // 2 // group, step, 0)

    def spread(c):
        pair_sum(c, 0)
        hops[c][0].start()
        if not CUTS[c][1]:
            hops[c][1].start()
        pair_sum(c, 1)
        hops[c][1 if CUTS[c][1] else 2].start()
        pair_sum(c, 2)
        hops[c][2 if CUTS[c][1] else 3].start()

    def forward(c):
        if CUTS[c][1]:
            return
        hops[c][0].wait_recv()
        add_far(c, 1, 0)
        hops[c][4].start()
        hops[c][1].wait_recv()
        add_far(c, 2, nb // 2)
        hops[c][5].start()

    def finish(c):
        pair_sum(c, 3)
        straight = CUTS[c][1]
        for hop in hops[c][0 if straight else 2:]:
            hop.wait_recv()

        def step(j, carry):
            blocks = pl.ds(j * group, group)
            summed = wide(own[c], 3, blocks) + wide(from_down[c], blocks) + wide(from_up[c], blocks)
            if straight:
                summed = summed + wide(far[c], blocks)
            grad[c][blocks] = summed.astype(jnp.bfloat16)
            return carry

        lax.fori_loop(0, nb // group, step, 0)

    def exchange(send, recv, at, ssem, rsem, fill_plane=None, fill=None, flat=False):
        mine = (at[0] * nf + me,) if flat else (*at, me)

        def plane(i, carry):
            px = (x + i) % nx
            if fill_plane is not None:
                fill_plane(px)
            for dz in order:
                p = px * nz + (z + dz) % nz
                if fill is not None:
                    fill(p)
                source, target = send.at[(*at, p)], recv.at[mine]
                if dz == 0:
                    @pl.when(i > 0)
                    def _():
                        remote(source, target, ssem, rsem, (d, p)).start()

                    @pl.when(i == 0)
                    def _():
                        recv[mine] = send[(*at, me)]
                else:
                    remote(source, target, ssem, rsem, (d, p)).start()
            return carry

        lax.fori_loop(0, nx, plane, 0)

    def arrived(ref, at, rsem, flat=False):
        whole = ref.at[pl.ds(at[0] * nf, nf - 1)] if flat else ref.at[(*at, pl.ds(0, nf - 1))]
        pltpu.make_async_copy(whole, whole, rsem).wait()

    def send_grad(c, stream):
        per = SLOTS if CUTS[c][2] else 1

        def fill(p):
            for i in range(per):
                g_send[c][stream, p, i] = grad[c][places[0, (stream * per + i) * nf + p]]

        exchange(g_send[c], g_recv[c], (stream,), g_ssem.at[c, stream], g_rsem.at[c, stream], fill=fill)

    streams = [range(1) if CUTS[c][2] else range(SLOTS) for c in range(NC)]
    span = nz * rows

    def product(c, s, t):
        at = (0, pl.ds(t * nz, nz), s) if CUTS[c][2] else (s, pl.ds(t * nz, nz), 0)
        held = g_recv[c][at].reshape(span, widths[c])
        return jnp.dot(held, right[s, cols[c], :], preferred_element_type=jnp.float32)

    def add_products(c, s):
        def step(t, carry):
            piece = pl.ds(t * span, span)
            made = product(c, s, t)
            if c > 0:
                made = total[s, piece] + made
            if c < NC - 1:
                total[s, piece] = made
            else:
                half[s, piece] = made.astype(jnp.bfloat16)
            return carry

        lax.fori_loop(0, nx, step, 0)

    spread(0)
    for c in range(1, NC):
        spread(c)
        if c == 1:
            find_places()
        finish(c - 1)
        for stream in streams[c - 1]:
            send_grad(c - 1, stream)
        forward(c)
    finish(NC - 1)
    for stream in streams[NC - 1]:
        send_grad(NC - 1, stream)

    for load in loads:
        load.wait()
    for s in range(SLOTS):
        for t in range(nx):
            piece = pl.ds(t * nz * rows, nz * rows)
            left_t[s, :, piece] = left[s, piece, :].T

    for c in range(NC - 1):
        for stream in streams[c]:
            arrived(g_recv[c], (stream,), g_rsem.at[c, stream])
        for s in range(SLOTS):
            add_products(c, s)

    for s in range(SLOTS):
        if s < len(streams[NC - 1]):
            arrived(g_recv[NC - 1], (s,), g_rsem.at[NC - 1, s])
        add_products(NC - 1, s)

        def rotate(px, s=s):
            made = jnp.dot(left_t[s, pl.ds(px * span, span)], half[s], preferred_element_type=jnp.float32)
            r_send[s, pl.ds(px * nz, nz)] = made.astype(jnp.bfloat16).reshape(nz, rows, columns)

        exchange(r_send, r_recv, (s,), r_ssem.at[s], r_rsem.at[s], fill_plane=rotate, flat=True)

    for s in range(SLOTS):
        arrived(r_recv, (s,), r_rsem.at[s], flat=True)

        def direct(p, s=s):
            block = places[0, s * nf + p]
            first_wide, second_wide = adam(r_recv[s * nf + p], first[block], second[block])
            d_send[s, p] = (first_wide / (jnp.sqrt(second_wide) + EPSILON)).astype(jnp.bfloat16)

        exchange(d_send, d_recv, (s,), d_ssem.at[s], d_rsem.at[s], fill=direct)

    def moments(j, carry):
        first_wide, second_wide = adam(r_recv[places[8, j]], first[j], second[j])
        first_new[j] = first_wide.astype(jnp.bfloat16)
        second_new[j] = second_wide
        return carry

    lax.fori_loop(0, nb, moments, 0)
    for s in range(SLOTS):
        arrived(d_recv, (s,), d_rsem.at[s])

        def undo_right(t, carry, s=s):
            held = d_recv[s, pl.ds(t * nz, nz)].reshape(span, columns)
            made = lax.dot_general(held, right[s], (((1,), (1,)), ((), ())), preferred_element_type=jnp.float32)
            back[s, pl.ds(t * span, span)] = made.astype(jnp.bfloat16)
            return carry

        lax.fori_loop(0, nx, undo_right, 0)

        def undo_left(px, s=s):
            made = jnp.dot(left[s, pl.ds(px * span, span)], back[s], preferred_element_type=jnp.float32)
            u_send[s, pl.ds(px * nz, nz)] = made.astype(jnp.bfloat16).reshape(nz, rows, columns)

        exchange(u_send, u_recv, (s,), u_ssem.at[s], u_rsem.at[s], fill_plane=undo_left, flat=True)

    for s in range(SLOTS):
        arrived(u_recv, (s,), u_rsem.at[s], flat=True)

    for c in range(NC):
        for r in range(NY):
            pairs[c][r].wait_send()
        for hop in hops[c]:
            hop.wait_send()
        for s in streams[c]:
            arrived(g_send[c], (s,), g_ssem.at[c, s])
    for s in range(SLOTS):
        arrived(r_send, (s,), r_ssem.at[s])
        arrived(d_send, (s,), d_ssem.at[s])
        arrived(u_send, (s,), u_ssem.at[s])


def deliver(places, first_new, second_new, u_recv, first_out, second_out, update_out, sem):
    outs = [
        pltpu.make_async_copy(first_new, first_out, sem.at[0]),
        pltpu.make_async_copy(second_new, second_out, sem.at[1]),
    ]
    for out in outs:
        out.start()

    def pick(j, carry):
        pltpu.make_async_copy(u_recv.at[places[8, j]], update_out.at[j], sem.at[2]).start()
        return carry

    lax.fori_loop(0, update_out.shape[0], pick, 0)
    for out in outs:
        out.wait()
    pltpu.make_async_copy(update_out, update_out, sem.at[2]).wait()


def per_device(nx, nz, grad_parts, first_moment, second_moment, left_basis, right_basis, owner_list):
    nf = nx * nz
    nb, rows, columns = first_moment.shape
    grads = grad_parts.reshape(NY, 2, nb, rows, columns)
    bf16, f32 = jnp.bfloat16, jnp.float32
    dma = pltpu.SemaphoreType.DMA
    order = nf * rows
    moved = pltpu.VMEM((SLOTS, nf, rows, columns), bf16)
    flat = pltpu.VMEM((SLOTS * nf, rows, columns), bf16)
    square = pltpu.VMEM((SLOTS, order, columns), bf16)
    hbm = pl.BlockSpec(memory_space=pl.ANY)
    smem = pl.BlockSpec(memory_space=pltpu.SMEM)
    cut_scratch = []
    for (_, _, merged), width in zip(CUTS, column_cuts(columns)[1]):
        part = pltpu.VMEM((NY, nb, rows, width), bf16)
        group = pltpu.VMEM((nb, rows, width), bf16)
        per = SLOTS if merged else 1
        sent = pltpu.VMEM((SLOTS // per, nf, per, rows, width), bf16)
        cut_scratch += [part, part, group, group, group, group, sent, sent]
    vmem = pl.BlockSpec(memory_space=pltpu.VMEM)

    def stay(array):
        return pltpu.with_memory_space_constraint(array, pltpu.HBM)

    first_new, second_new, u_recv, table = pl.pallas_call(
        functools.partial(kernel, nx, nz),
        out_shape=(
            pltpu.VMEM((nb, rows, columns), bf16),
            pltpu.VMEM((nb, rows, columns), f32),
            pltpu.VMEM((SLOTS * nf, rows, columns), bf16),
            pltpu.VMEM((16, 128), jnp.int32),
        ),
        in_specs=[smem, hbm, hbm, hbm, hbm, hbm],
        out_specs=(vmem, vmem, vmem, vmem),
        scratch_shapes=cut_scratch + [
            pltpu.SMEM((16, 128), jnp.int32),
            moved, flat, moved, moved, moved,
            pltpu.VMEM((nb, rows, columns), bf16),
            pltpu.VMEM((nb, rows, columns), f32),
            square, square, square,
            pltpu.VMEM((SLOTS, order, columns), f32),
            square, square,
            dma((5,)), dma((NC, NY)), dma((NC, NY)), dma((NC, NY)), dma((NC, 6)), dma((NC, 6)),
            dma((NC, SLOTS)), dma((NC, SLOTS)),
            dma((SLOTS,)), dma((SLOTS,)), dma((SLOTS,)), dma((SLOTS,)), dma((SLOTS,)), dma((SLOTS,)),
        ],
        compiler_params=pltpu.CompilerParams(
            collective_id=0, has_side_effects=True, vmem_limit_bytes=VMEM_BYTES
        ),
        cost_estimate=pl.CostEstimate(
            flops=SLOTS * 8 * order * columns * columns, bytes_accessed=16 * 1024 * 1024, transcendentals=0
        ),
    )(
        stay(owner_list.reshape(nb)), stay(grads), stay(first_moment), stay(second_moment),
        stay(left_basis.reshape(SLOTS, order, order)), stay(right_basis.reshape(SLOTS, columns, columns)),
    )
    return pl.pallas_call(
        deliver,
        out_shape=(
            jax.ShapeDtypeStruct((nb, rows, columns), bf16),
            jax.ShapeDtypeStruct((nb, rows, columns), f32),
            jax.ShapeDtypeStruct((nb, rows, columns), bf16),
        ),
        in_specs=[smem, vmem, vmem, vmem],
        out_specs=(hbm, hbm, hbm),
        scratch_shapes=[dma((3,))],
    )(table, first_new, second_new, u_recv)


def solution(mesh):
    nf = mesh.shape["fsdp"]
    nz = min(8, nf // 2)
    placed = (
        P("dp", None, "fsdp", None),
        P("dp", "fsdp", None),
        P("dp", "fsdp", None),
        P("dp", "fsdp", None, None, None),
        P("dp", "fsdp", None, None, None),
        P("dp", None, None),
    )
    return jax.shard_map(
        functools.partial(per_device, nf // nz, nz),
        mesh=mesh,
        in_specs=placed,
        out_specs=(P("dp", "fsdp", None), P("dp", "fsdp", None), P("dp", "fsdp", None)),
        check_vma=False,
    )
```

```python
import functools

import jax
import jax.numpy as jnp
from jax import lax
from jax.experimental import pallas as pl
from jax.experimental.pallas import tpu as pltpu
from jax.sharding import PartitionSpec as P

BETA_FIRST = 0.9
BETA_SECOND = 0.95
EPSILON = 1e-08

MESH = pl.DeviceIdType.MESH
VMEM_BYTES = 32 * 1024 * 1024
DELIVER_VMEM_BYTES = 8 * 1024 * 1024
NY = 4
SLOTS = 2
CUTS = ((2, False, True), (2, False, True), (2, False, True), (2, False, False))
NC = len(CUTS)


def column_cuts(columns):
    widths = [columns * eighths // 8 for eighths, _, _ in CUTS]
    return [sum(widths[:c]) for c in range(NC)], widths


def z_order(nz):
    order = [0]
    for step in range(1, nz // 2 + 1):
        order.append(step)
        if nz - step != step:
            order.append(nz - step)
    return order[::-1]


def adam(rotated, first, second):
    wide = rotated.astype(jnp.float32)
    first_wide = BETA_FIRST * first.astype(jnp.float32) + (1.0 - BETA_FIRST) * wide
    second_new = BETA_SECOND * second + (1.0 - BETA_SECOND) * wide * wide
    return first_wide, second_new


def kernel(
    nx, nz,
    owners, grads, first_hbm, second_hbm, left_hbm, right_hbm,
    first_new, second_new, update,
    *scratch,
):
    cut_refs = [scratch[c * 8:c * 8 + 8] for c in range(NC)]
    own, other, far, from_down, from_up, grad, g_send, g_recv = zip(*cut_refs)
    (
        table, named_blocks, places,
        r_send, r_recv, d_send, d_recv, u_send, u_recv,
        first, second, left, right, left_t, total, half, back,
        load_sem, own_sem, pair_send, pair_recv, y_send, y_recv,
        g_ssem, g_rsem, r_ssem, r_rsem, d_ssem, d_rsem, u_ssem, u_rsem,
    ) = scratch[NC * 8:]
    nf = nx * nz
    nb, rows, columns = first.shape
    starts, widths = column_cuts(columns)
    d, me = lax.axis_index("dp"), lax.axis_index("fsdp")
    y, core = d // 2, d % 2
    x, z = me // nz, me % nz
    up, down = (y + 1) % NY, (y + NY - 1) % NY
    at_up, at_down, at_pair = (up * 2 + core, me), (down * 2 + core, me), (y * 2 + 1 - core, me)
    at_far = (((y + 2) % NY) * 2 + core, me)
    order = z_order(nz)

    chips = [(y + 2) % NY, up, down, y]
    loads = [
        pltpu.make_async_copy(ref, to, load_sem.at[i])
        for i, (ref, to) in enumerate(
            [(left_hbm, left), (right_hbm, right), (first_hbm, first), (second_hbm, second)]
        )
    ]
    cols = [pl.ds(starts[c], widths[c]) for c in range(NC)]
    owns = [
        [
            pltpu.make_async_copy(grads.at[chips[r], core, :, :, cols[c]], own[c].at[r], own_sem.at[c, r])
            for r in range(NY)
        ]
        for c in range(NC)
    ]
    owner_load = pltpu.make_async_copy(owners, named_blocks, load_sem.at[5])
    owner_load.start()
    for r in range(NY):
        owns[0][r].start()

    def find_places():
        owner_load.wait()
        lane = lax.broadcasted_iota(jnp.int32, (8, 128), 1)
        zero = jnp.zeros((8, 128), jnp.int32)

        def step(j, carry):
            count, source, named = carry
            owner = named_blocks[j]
            match = lane % nf == owner
            source = jnp.where(jnp.logical_and(match, count == lane // nf), j, source)
            return count + match.astype(jnp.int32), source, jnp.where(lane == j, owner, named)

        _, source, named = lax.fori_loop(0, nb, step, (zero, zero, zero))

        def earlier(i, slot):
            return slot + jnp.logical_and(named == named_blocks[i], lane > i).astype(jnp.int32)

        table[0:8] = source
        table[8:16] = jnp.minimum(lax.fori_loop(0, nb, earlier, zero), SLOTS - 1) * nf + named
        copy = pltpu.make_async_copy(table, places, load_sem.at[4])
        copy.start()
        copy.wait()

    barrier = pltpu.get_barrier_semaphore()

    def greet(i, carry):
        for dz in order:
            p = ((x + i) % nx) * nz + (z + dz) % nz
            if dz == 0:
                @pl.when(i > 0)
                def _():
                    pl.semaphore_signal(barrier, inc=1, device_id=(d, p), device_id_type=MESH)
            else:
                pl.semaphore_signal(barrier, inc=1, device_id=(d, p), device_id_type=MESH)
        return carry

    for device in (at_pair, at_far, at_up, at_down):
        pl.semaphore_signal(barrier, inc=1, device_id=device, device_id_type=MESH)
    lax.fori_loop(0, nx, greet, 0)
    pl.semaphore_wait(barrier, nf - 1 + 4)

    def remote(source, target, send, recv, device):
        return pltpu.make_async_remote_copy(
            src_ref=source, dst_ref=target, send_sem=send, recv_sem=recv, device_id=device, device_id_type=MESH
        )

    pairs = [
        [
            remote(
                grads.at[chips[r], 1 - core, :, :, cols[c]], other[c].at[r],
                pair_send.at[c, r], pair_recv.at[c, r], at_pair,
            )
            for r in range(NY)
        ]
        for c in range(NC)
    ]
    for c in range(NC):
        for r in range(NY):
            pairs[c][r].start()
            if c > 0:
                owns[c][r].start()
    for load in loads:
        load.start()

    low, high = pl.ds(0, nb // 2), pl.ds(nb // 2, nb // 2)

    def y_hop(c, i, source, target, device):
        return remote(source, target, y_send.at[c, i], y_recv.at[c, i], device)

    hops = [
        [
            y_hop(c, 0, own[c].at[0], far[c], at_far),
            y_hop(c, 1, own[c].at[1], from_down[c], at_up),
            y_hop(c, 2, own[c].at[2], from_up[c], at_down),
        ]
        if CUTS[c][1]
        else [
            y_hop(c, 0, own[c].at[0, low], far[c].at[low], at_up),
            y_hop(c, 1, own[c].at[0, high], far[c].at[high], at_down),
            y_hop(c, 2, own[c].at[1, high], from_down[c].at[high], at_up),
            y_hop(c, 3, own[c].at[2, low], from_up[c].at[low], at_down),
            y_hop(c, 4, own[c].at[1, low], from_down[c].at[low], at_up),
            y_hop(c, 5, own[c].at[2, high], from_up[c].at[high], at_down),
        ]
        for c in range(NC)
    ]
    group = min(4, nb // 2)

    def wide(ref, *at):
        return ref[at].astype(jnp.float32)

    def pair_sum(c, r):
        owns[c][r].wait()
        pairs[c][r].wait_recv()

        def step(j, carry):
            blocks = pl.ds(j * group, group)
            own[c][r, blocks] = (wide(own[c], r, blocks) + wide(other[c], r, blocks)).astype(jnp.bfloat16)
            return carry

        lax.fori_loop(0, nb // group, step, 0)

    def add_far(c, r, first_block):
        def step(j, carry):
            blocks = pl.ds(first_block + j * group, group)
            own[c][r, blocks] = (wide(own[c], r, blocks) + wide(far[c], blocks)).astype(jnp.bfloat16)
            return carry

        lax.fori_loop(0, nb // 2 // group, step, 0)

    def spread(c):
        pair_sum(c, 0)
        hops[c][0].start()
        if not CUTS[c][1]:
            hops[c][1].start()
        pair_sum(c, 1)
        hops[c][1 if CUTS[c][1] else 2].start()
        pair_sum(c, 2)
        hops[c][2 if CUTS[c][1] else 3].start()

    def forward(c):
        if CUTS[c][1]:
            return
        hops[c][0].wait_recv()
        add_far(c, 1, 0)
        hops[c][4].start()
        hops[c][1].wait_recv()
        add_far(c, 2, nb // 2)
        hops[c][5].start()

    def finish(c):
        pair_sum(c, 3)
        straight = CUTS[c][1]
        for hop in hops[c][0 if straight else 2:]:
            hop.wait_recv()

        def step(j, carry):
            blocks = pl.ds(j * group, group)
            summed = wide(own[c], 3, blocks) + wide(from_down[c], blocks) + wide(from_up[c], blocks)
            if straight:
                summed = summed + wide(far[c], blocks)
            grad[c][blocks] = summed.astype(jnp.bfloat16)
            return carry

        lax.fori_loop(0, nb // group, step, 0)

    def exchange(send, recv, at, ssem, rsem, fill_plane=None, fill=None, flat=False):
        mine = (at[0] * nf + me,) if flat else (*at, me)

        def plane(i, carry):
            px = (x + nx // 2 + i) % nx
            if fill_plane is not None:
                fill_plane(px)
            for dz in order:
                p = px * nz + (z + dz) % nz
                if fill is not None:
                    fill(p)
                source, target = send.at[(*at, p)], recv.at[mine]
                if dz == 0:
                    @pl.when(i != nx - nx // 2)
                    def _():
                        remote(source, target, ssem, rsem, (d, p)).start()

                    @pl.when(i == nx - nx // 2)
                    def _():
                        recv[mine] = send[(*at, me)]
                else:
                    remote(source, target, ssem, rsem, (d, p)).start()
            return carry

        lax.fori_loop(0, nx, plane, 0)

    def arrived(ref, at, rsem, flat=False):
        whole = ref.at[pl.ds(at[0] * nf, nf - 1)] if flat else ref.at[(*at, pl.ds(0, nf - 1))]
        pltpu.make_async_copy(whole, whole, rsem).wait()

    def send_grad(c, stream):
        per = SLOTS if CUTS[c][2] else 1

        def fill(p):
            for i in range(per):
                g_send[c][stream, p, i] = grad[c][places[0, (stream * per + i) * nf + p]]

        exchange(g_send[c], g_recv[c], (stream,), g_ssem.at[c, stream], g_rsem.at[c, stream], fill=fill)

    streams = [range(1) if CUTS[c][2] else range(SLOTS) for c in range(NC)]
    span = nz * rows

    def product(c, s, t):
        at = (0, pl.ds(t * nz, nz), s) if CUTS[c][2] else (s, pl.ds(t * nz, nz), 0)
        held = g_recv[c][at].reshape(span, widths[c])
        return jnp.dot(held, right[s, cols[c], :], preferred_element_type=jnp.float32)

    def add_products(c, s):
        def step(t, carry):
            piece = pl.ds(t * span, span)
            made = product(c, s, t)
            if c > 0:
                made = total[s, piece] + made
            if c < NC - 1:
                total[s, piece] = made
            else:
                half[s, piece] = made.astype(jnp.bfloat16)
            return carry

        lax.fori_loop(0, nx, step, 0)

    spread(0)
    for c in range(1, NC):
        if c == 1:
            find_places()
        forward(c - 1)
        spread(c)
        finish(c - 1)
        for stream in streams[c - 1]:
            send_grad(c - 1, stream)
    forward(NC - 1)
    finish(NC - 1)
    for stream in streams[NC - 1]:
        send_grad(NC - 1, stream)

    for load in loads:
        load.wait()
    for s in range(SLOTS):
        for t in range(nx):
            piece = pl.ds(t * nz * rows, nz * rows)
            left_t[s, :, piece] = left[s, piece, :].T

    for c in range(NC - 1):
        for stream in streams[c]:
            arrived(g_recv[c], (stream,), g_rsem.at[c, stream])
        for s in range(SLOTS):
            add_products(c, s)

    for s in range(SLOTS):
        if s < len(streams[NC - 1]):
            arrived(g_recv[NC - 1], (s,), g_rsem.at[NC - 1, s])
        add_products(NC - 1, s)

        def rotate(px, s=s):
            made = jnp.dot(left_t[s, pl.ds(px * span, span)], half[s], preferred_element_type=jnp.float32)
            r_send[s, pl.ds(px * nz, nz)] = made.astype(jnp.bfloat16).reshape(nz, rows, columns)

        exchange(r_send, r_recv, (s,), r_ssem.at[s], r_rsem.at[s], fill_plane=rotate, flat=True)

    for s in range(SLOTS):
        arrived(r_recv, (s,), r_rsem.at[s], flat=True)

        def direct(p, s=s):
            block = places[0, s * nf + p]
            first_wide, second_wide = adam(r_recv[s * nf + p], first[block], second[block])
            d_send[s, p] = (first_wide / (jnp.sqrt(second_wide) + EPSILON)).astype(jnp.bfloat16)

        exchange(d_send, d_recv, (s,), d_ssem.at[s], d_rsem.at[s], fill=direct)

    def moments(j, carry):
        first_wide, second_wide = adam(r_recv[places[8, j]], first[j], second[j])
        first_new[j] = first_wide.astype(jnp.bfloat16)
        second_new[j] = second_wide
        return carry

    lax.fori_loop(0, nb, moments, 0)
    for s in range(SLOTS):
        arrived(d_recv, (s,), d_rsem.at[s])

        def undo_right(t, carry, s=s):
            held = d_recv[s, pl.ds(t * nz, nz)].reshape(span, columns)
            made = lax.dot_general(held, right[s], (((1,), (1,)), ((), ())), preferred_element_type=jnp.float32)
            back[s, pl.ds(t * span, span)] = made.astype(jnp.bfloat16)
            return carry

        lax.fori_loop(0, nx, undo_right, 0)

        def undo_left(px, s=s):
            made = jnp.dot(left[s, pl.ds(px * span, span)], back[s], preferred_element_type=jnp.float32)
            u_send[s, pl.ds(px * nz, nz)] = made.astype(jnp.bfloat16).reshape(nz, rows, columns)

        exchange(u_send, u_recv, (s,), u_ssem.at[s], u_rsem.at[s], fill_plane=undo_left, flat=True)

    for s in range(SLOTS):
        arrived(u_recv, (s,), u_rsem.at[s], flat=True)

    def pick(j, carry):
        update[j] = u_recv[places[8, j]]
        return carry

    lax.fori_loop(0, nb, pick, 0)

    for c in range(NC):
        for r in range(NY):
            pairs[c][r].wait_send()
        for hop in hops[c]:
            hop.wait_send()
        for s in streams[c]:
            arrived(g_send[c], (s,), g_ssem.at[c, s])
    for s in range(SLOTS):
        arrived(r_send, (s,), r_ssem.at[s])
        arrived(d_send, (s,), d_ssem.at[s])
        arrived(u_send, (s,), u_ssem.at[s])


def deliver(*refs):
    count = (len(refs) - 1) // 2
    copies = [pltpu.make_async_copy(refs[i], refs[count + i], refs[-1].at[i]) for i in range(count)]
    for copy in copies:
        copy.start()
    for copy in copies:
        copy.wait()


def per_device(nx, nz, grad_parts, first_moment, second_moment, left_basis, right_basis, owner_list):
    nf = nx * nz
    nb, rows, columns = first_moment.shape
    grads = grad_parts.reshape(NY, 2, nb, rows, columns)
    bf16, f32 = jnp.bfloat16, jnp.float32
    dma = pltpu.SemaphoreType.DMA
    order = nf * rows
    moved = pltpu.VMEM((SLOTS, nf, rows, columns), bf16)
    flat = pltpu.VMEM((SLOTS * nf, rows, columns), bf16)
    square = pltpu.VMEM((SLOTS, order, columns), bf16)
    hbm = pl.BlockSpec(memory_space=pl.ANY)
    cut_scratch = []
    for (_, _, merged), width in zip(CUTS, column_cuts(columns)[1]):
        part = pltpu.VMEM((NY, nb, rows, width), bf16)
        group = pltpu.VMEM((nb, rows, width), bf16)
        per = SLOTS if merged else 1
        sent = pltpu.VMEM((SLOTS // per, nf, per, rows, width), bf16)
        cut_scratch += [part, part, group, group, group, group, sent, sent]
    vmem = pl.BlockSpec(memory_space=pltpu.VMEM)

    def stay(array):
        return pltpu.with_memory_space_constraint(array, pltpu.HBM)

    made = pl.pallas_call(
        functools.partial(kernel, nx, nz),
        out_shape=(
            pltpu.VMEM((nb, rows, columns), bf16),
            pltpu.VMEM((nb, rows, columns), f32),
            pltpu.VMEM((nb, rows, columns), bf16),
        ),
        in_specs=[hbm, hbm, hbm, hbm, hbm, hbm],
        out_specs=(vmem, vmem, vmem),
        scratch_shapes=cut_scratch + [
            pltpu.VMEM((16, 128), jnp.int32), pltpu.SMEM((nb,), jnp.int32), pltpu.SMEM((16, 128), jnp.int32),
            moved, flat, moved, moved, moved, flat,
            pltpu.VMEM((nb, rows, columns), bf16),
            pltpu.VMEM((nb, rows, columns), f32),
            square, square, square,
            pltpu.VMEM((SLOTS, order, columns), f32),
            square, square,
            dma((6,)), dma((NC, NY)), dma((NC, NY)), dma((NC, NY)), dma((NC, 6)), dma((NC, 6)),
            dma((NC, SLOTS)), dma((NC, SLOTS)),
            dma((SLOTS,)), dma((SLOTS,)), dma((SLOTS,)), dma((SLOTS,)), dma((SLOTS,)), dma((SLOTS,)),
        ],
        compiler_params=pltpu.CompilerParams(
            collective_id=0, has_side_effects=True, vmem_limit_bytes=VMEM_BYTES
        ),
        cost_estimate=pl.CostEstimate(
            flops=SLOTS * 8 * order * columns * columns, bytes_accessed=16 * 1024 * 1024, transcendentals=0
        ),
    )(
        stay(owner_list.reshape(nb)), stay(grads), stay(first_moment), stay(second_moment),
        stay(left_basis.reshape(SLOTS, order, order)), stay(right_basis.reshape(SLOTS, columns, columns)),
    )
    return pl.pallas_call(
        deliver,
        out_shape=(
            jax.ShapeDtypeStruct((nb, rows, columns), bf16),
            jax.ShapeDtypeStruct((nb, rows, columns), f32),
            jax.ShapeDtypeStruct((nb, rows, columns), bf16),
        ),
        in_specs=[vmem, vmem, vmem],
        out_specs=(hbm, hbm, hbm),
        scratch_shapes=[dma((3,))],
        compiler_params=pltpu.CompilerParams(vmem_limit_bytes=DELIVER_VMEM_BYTES),
    )(*(pltpu.with_memory_space_constraint(array, pltpu.VMEM) for array in made))


def solution(mesh):
    nf = mesh.shape["fsdp"]
    nz = min(8, nf // 2)
    placed = (
        P("dp", None, "fsdp", None),
        P("dp", "fsdp", None),
        P("dp", "fsdp", None),
        P("dp", "fsdp", None, None, None),
        P("dp", "fsdp", None, None, None),
        P("dp", None, None),
    )
    return jax.shard_map(
        functools.partial(per_device, nf // nz, nz),
        mesh=mesh,
        in_specs=placed,
        out_specs=(P("dp", "fsdp", None), P("dp", "fsdp", None), P("dp", "fsdp", None)),
        check_vma=False,
    )
```

```python
import functools

import jax
import jax.numpy as jnp
from jax import lax
from jax.experimental import pallas as pl
from jax.experimental.pallas import tpu as pltpu
from jax.sharding import PartitionSpec as P

BETA_FIRST = 0.9
BETA_SECOND = 0.95
EPSILON = 1e-08

MESH = pl.DeviceIdType.MESH
VMEM_BYTES = 32 * 1024 * 1024
DELIVER_VMEM_BYTES = 8 * 1024 * 1024
NY = 4
SLOTS = 2
CUTS = ((2, False, True), (2, False, True), (2, False, True), (2, False, False))
NC = len(CUTS)


def column_cuts(columns):
    widths = [columns * eighths // 8 for eighths, _, _ in CUTS]
    return [sum(widths[:c]) for c in range(NC)], widths


def z_order(nz):
    order = [0]
    for step in range(1, nz // 2 + 1):
        order.append(step)
        if nz - step != step:
            order.append(nz - step)
    return order[::-1]


def adam(rotated, first, second):
    wide = rotated.astype(jnp.float32)
    first_wide = BETA_FIRST * first.astype(jnp.float32) + (1.0 - BETA_FIRST) * wide
    second_new = BETA_SECOND * second + (1.0 - BETA_SECOND) * wide * wide
    return first_wide, second_new


def kernel(
    nx, nz,
    owners, grads, first_hbm, second_hbm, left_hbm, right_hbm,
    first_new, second_new, update,
    *scratch,
):
    cut_refs = [scratch[c * 8:c * 8 + 8] for c in range(NC)]
    own, other, far, from_down, from_up, grad, g_send, g_recv = zip(*cut_refs)
    (
        table, named_blocks, places,
        r_send, r_recv, d_send, d_recv, u_send, u_recv,
        first, second, left, right, left_t, total, half, back,
        load_sem, own_sem, pair_send, pair_recv, y_send, y_recv,
        g_ssem, g_rsem, r_ssem, r_rsem, d_ssem, d_rsem, u_ssem, u_rsem, round_sem,
    ) = scratch[NC * 8:]
    nf = nx * nz
    nb, rows, columns = first.shape
    starts, widths = column_cuts(columns)
    d, me = lax.axis_index("dp"), lax.axis_index("fsdp")
    y, core = d // 2, d % 2
    x, z = me // nz, me % nz
    up, down = (y + 1) % NY, (y + NY - 1) % NY
    at_up, at_down, at_pair = (up * 2 + core, me), (down * 2 + core, me), (y * 2 + 1 - core, me)
    at_far = (((y + 2) % NY) * 2 + core, me)
    order = z_order(nz)

    chips = [(y + 2) % NY, up, down, y]
    loads = [
        pltpu.make_async_copy(ref, to, load_sem.at[i])
        for i, (ref, to) in enumerate(
            [(left_hbm, left), (right_hbm, right), (first_hbm, first), (second_hbm, second)]
        )
    ]
    cols = [pl.ds(starts[c], widths[c]) for c in range(NC)]
    owns = [
        [
            pltpu.make_async_copy(grads.at[chips[r], core, :, :, cols[c]], own[c].at[r], own_sem.at[c, r])
            for r in range(NY)
        ]
        for c in range(NC)
    ]
    owner_load = pltpu.make_async_copy(owners, named_blocks, load_sem.at[5])
    owner_load.start()
    for r in range(NY):
        owns[0][r].start()

    def find_places():
        owner_load.wait()
        lane = lax.broadcasted_iota(jnp.int32, (8, 128), 1)
        zero = jnp.zeros((8, 128), jnp.int32)

        def step(j, carry):
            count, source, named = carry
            owner = named_blocks[j]
            match = lane % nf == owner
            source = jnp.where(jnp.logical_and(match, count == lane // nf), j, source)
            return count + match.astype(jnp.int32), source, jnp.where(lane == j, owner, named)

        _, source, named = lax.fori_loop(0, nb, step, (zero, zero, zero))

        def earlier(i, slot):
            return slot + jnp.logical_and(named == named_blocks[i], lane > i).astype(jnp.int32)

        table[0:8] = source
        table[8:16] = jnp.minimum(lax.fori_loop(0, nb, earlier, zero), SLOTS - 1) * nf + named
        copy = pltpu.make_async_copy(table, places, load_sem.at[4])
        copy.start()
        copy.wait()

    barrier = pltpu.get_barrier_semaphore()

    def across(dx, dz):
        return d, ((x + nx + dx) % nx) * nz + (z + nz + dz) % nz

    near = [at_pair, at_far, at_up, at_down, across(0, 1), across(0, -1), across(1, 0), across(-1, 0)]
    for device in near:
        pl.semaphore_signal(barrier, inc=1, device_id=device, device_id_type=MESH)
    pl.semaphore_wait(barrier, len(near))

    rounds = [[(0, 1), (0, -1)], [(0, 2), (0, -2)]] if nz > 2 else []
    rounds.append([(1, 0), (-1, 0)])
    if nx > 2:
        rounds.append([(2, 0)])

    def tell(k):
        for dx, dz in rounds[k]:
            pl.semaphore_signal(round_sem.at[k], inc=1, device_id=across(dx, dz), device_id_type=MESH)

    def hear(k):
        if k < len(rounds):
            pl.semaphore_wait(round_sem.at[k], len(rounds[k]))
            if k + 1 < len(rounds):
                tell(k + 1)

    tell(0)

    def remote(source, target, send, recv, device):
        return pltpu.make_async_remote_copy(
            src_ref=source, dst_ref=target, send_sem=send, recv_sem=recv, device_id=device, device_id_type=MESH
        )

    pairs = [
        [
            remote(
                grads.at[chips[r], 1 - core, :, :, cols[c]], other[c].at[r],
                pair_send.at[c, r], pair_recv.at[c, r], at_pair,
            )
            for r in range(NY)
        ]
        for c in range(NC)
    ]
    for c in range(NC):
        for r in range(NY):
            pairs[c][r].start()
            if c > 0:
                owns[c][r].start()
    for load in loads:
        load.start()

    low, high = pl.ds(0, nb // 2), pl.ds(nb // 2, nb // 2)

    def y_hop(c, i, source, target, device):
        return remote(source, target, y_send.at[c, i], y_recv.at[c, i], device)

    hops = [
        [
            y_hop(c, 0, own[c].at[0], far[c], at_far),
            y_hop(c, 1, own[c].at[1], from_down[c], at_up),
            y_hop(c, 2, own[c].at[2], from_up[c], at_down),
        ]
        if CUTS[c][1]
        else [
            y_hop(c, 0, own[c].at[0, low], far[c].at[low], at_up),
            y_hop(c, 1, own[c].at[0, high], far[c].at[high], at_down),
            y_hop(c, 2, own[c].at[1, high], from_down[c].at[high], at_up),
            y_hop(c, 3, own[c].at[2, low], from_up[c].at[low], at_down),
            y_hop(c, 4, own[c].at[1, low], from_down[c].at[low], at_up),
            y_hop(c, 5, own[c].at[2, high], from_up[c].at[high], at_down),
        ]
        for c in range(NC)
    ]
    group = min(4, nb // 2)

    def wide(ref, *at):
        return ref[at].astype(jnp.float32)

    def pair_sum(c, r):
        owns[c][r].wait()
        pairs[c][r].wait_recv()

        def step(j, carry):
            blocks = pl.ds(j * group, group)
            own[c][r, blocks] = (wide(own[c], r, blocks) + wide(other[c], r, blocks)).astype(jnp.bfloat16)
            return carry

        lax.fori_loop(0, nb // group, step, 0)

    def add_far(c, r, first_block):
        def step(j, carry):
            blocks = pl.ds(first_block + j * group, group)
            own[c][r, blocks] = (wide(own[c], r, blocks) + wide(far[c], blocks)).astype(jnp.bfloat16)
            return carry

        lax.fori_loop(0, nb // 2 // group, step, 0)

    def spread(c):
        pair_sum(c, 0)
        hops[c][0].start()
        if not CUTS[c][1]:
            hops[c][1].start()
        pair_sum(c, 1)
        hops[c][1 if CUTS[c][1] else 2].start()
        pair_sum(c, 2)
        hops[c][2 if CUTS[c][1] else 3].start()

    def forward(c):
        if CUTS[c][1]:
            return
        hops[c][0].wait_recv()
        add_far(c, 1, 0)
        hops[c][4].start()
        hops[c][1].wait_recv()
        add_far(c, 2, nb // 2)
        hops[c][5].start()

    def finish(c):
        pair_sum(c, 3)
        straight = CUTS[c][1]
        for hop in hops[c][0 if straight else 2:]:
            hop.wait_recv()

        def step(j, carry):
            blocks = pl.ds(j * group, group)
            summed = wide(own[c], 3, blocks) + wide(from_down[c], blocks) + wide(from_up[c], blocks)
            if straight:
                summed = summed + wide(far[c], blocks)
            grad[c][blocks] = summed.astype(jnp.bfloat16)
            return carry

        lax.fori_loop(0, nb // group, step, 0)

    def exchange(send, recv, at, ssem, rsem, fill_plane=None, fill=None, flat=False):
        mine = (at[0] * nf + me,) if flat else (*at, me)

        def plane(i, carry):
            px = (x + nx // 2 + i) % nx
            if fill_plane is not None:
                fill_plane(px)
            for dz in order:
                p = px * nz + (z + dz) % nz
                if fill is not None:
                    fill(p)
                source, target = send.at[(*at, p)], recv.at[mine]
                if dz == 0:
                    @pl.when(i != nx - nx // 2)
                    def _():
                        remote(source, target, ssem, rsem, (d, p)).start()

                    @pl.when(i == nx - nx // 2)
                    def _():
                        recv[mine] = send[(*at, me)]
                else:
                    remote(source, target, ssem, rsem, (d, p)).start()
            return carry

        lax.fori_loop(0, nx, plane, 0)

    def arrived(ref, at, rsem, flat=False):
        whole = ref.at[pl.ds(at[0] * nf, nf - 1)] if flat else ref.at[(*at, pl.ds(0, nf - 1))]
        pltpu.make_async_copy(whole, whole, rsem).wait()

    def send_grad(c, stream):
        per = SLOTS if CUTS[c][2] else 1

        def fill(p):
            for i in range(per):
                g_send[c][stream, p, i] = grad[c][places[0, (stream * per + i) * nf + p]]

        exchange(g_send[c], g_recv[c], (stream,), g_ssem.at[c, stream], g_rsem.at[c, stream], fill=fill)

    streams = [range(1) if CUTS[c][2] else range(SLOTS) for c in range(NC)]
    span = nz * rows

    def product(c, s, t):
        at = (0, pl.ds(t * nz, nz), s) if CUTS[c][2] else (s, pl.ds(t * nz, nz), 0)
        held = g_recv[c][at].reshape(span, widths[c])
        return jnp.dot(held, right[s, cols[c], :], preferred_element_type=jnp.float32)

    def add_products(c, s):
        def step(t, carry):
            piece = pl.ds(t * span, span)
            made = product(c, s, t)
            if c > 0:
                made = total[s, piece] + made
            if c < NC - 1:
                total[s, piece] = made
            else:
                half[s, piece] = made.astype(jnp.bfloat16)
            return carry

        lax.fori_loop(0, nx, step, 0)

    hear(0)
    spread(0)
    for c in range(1, NC):
        if c == 1:
            hear(1)
            find_places()
            hear(2)
        forward(c - 1)
        if c == 1:
            hear(3)
        spread(c)
        finish(c - 1)
        for stream in streams[c - 1]:
            send_grad(c - 1, stream)
    forward(NC - 1)
    finish(NC - 1)
    for stream in streams[NC - 1]:
        send_grad(NC - 1, stream)

    for load in loads:
        load.wait()
    for s in range(SLOTS):
        for t in range(nx):
            piece = pl.ds(t * nz * rows, nz * rows)
            left_t[s, :, piece] = left[s, piece, :].T

    for c in range(NC - 1):
        for stream in streams[c]:
            arrived(g_recv[c], (stream,), g_rsem.at[c, stream])
        for s in range(SLOTS):
            add_products(c, s)

    for s in range(SLOTS):
        if s < len(streams[NC - 1]):
            arrived(g_recv[NC - 1], (s,), g_rsem.at[NC - 1, s])
        add_products(NC - 1, s)

        def rotate(px, s=s):
            made = jnp.dot(left_t[s, pl.ds(px * span, span)], half[s], preferred_element_type=jnp.float32)
            r_send[s, pl.ds(px * nz, nz)] = made.astype(jnp.bfloat16).reshape(nz, rows, columns)

        exchange(r_send, r_recv, (s,), r_ssem.at[s], r_rsem.at[s], fill_plane=rotate, flat=True)

    for s in range(SLOTS):
        arrived(r_recv, (s,), r_rsem.at[s], flat=True)

        def direct(p, s=s):
            block = places[0, s * nf + p]
            first_wide, second_wide = adam(r_recv[s * nf + p], first[block], second[block])
            d_send[s, p] = (first_wide / (jnp.sqrt(second_wide) + EPSILON)).astype(jnp.bfloat16)

        exchange(d_send, d_recv, (s,), d_ssem.at[s], d_rsem.at[s], fill=direct)

    def moments(j, carry):
        first_wide, second_wide = adam(r_recv[places[8, j]], first[j], second[j])
        first_new[j] = first_wide.astype(jnp.bfloat16)
        second_new[j] = second_wide
        return carry

    lax.fori_loop(0, nb, moments, 0)
    for s in range(SLOTS):
        arrived(d_recv, (s,), d_rsem.at[s])

        def undo_right(t, carry, s=s):
            held = d_recv[s, pl.ds(t * nz, nz)].reshape(span, columns)
            made = lax.dot_general(held, right[s], (((1,), (1,)), ((), ())), preferred_element_type=jnp.float32)
            back[s, pl.ds(t * span, span)] = made.astype(jnp.bfloat16)
            return carry

        lax.fori_loop(0, nx, undo_right, 0)

        def undo_left(px, s=s):
            made = jnp.dot(left[s, pl.ds(px * span, span)], back[s], preferred_element_type=jnp.float32)
            u_send[s, pl.ds(px * nz, nz)] = made.astype(jnp.bfloat16).reshape(nz, rows, columns)

        exchange(u_send, u_recv, (s,), u_ssem.at[s], u_rsem.at[s], fill_plane=undo_left, flat=True)

    for s in range(SLOTS):
        arrived(u_recv, (s,), u_rsem.at[s], flat=True)

    def pick(j, carry):
        update[j] = u_recv[places[8, j]]
        return carry

    lax.fori_loop(0, nb, pick, 0)

    for c in range(NC):
        for r in range(NY):
            pairs[c][r].wait_send()
        for hop in hops[c]:
            hop.wait_send()
        for s in streams[c]:
            arrived(g_send[c], (s,), g_ssem.at[c, s])
    for s in range(SLOTS):
        arrived(r_send, (s,), r_ssem.at[s])
        arrived(d_send, (s,), d_ssem.at[s])
        arrived(u_send, (s,), u_ssem.at[s])


def deliver(*refs):
    count = (len(refs) - 1) // 2
    copies = [pltpu.make_async_copy(refs[i], refs[count + i], refs[-1].at[i]) for i in range(count)]
    for copy in copies:
        copy.start()
    for copy in copies:
        copy.wait()


def per_device(nx, nz, grad_parts, first_moment, second_moment, left_basis, right_basis, owner_list):
    nf = nx * nz
    nb, rows, columns = first_moment.shape
    grads = grad_parts.reshape(NY, 2, nb, rows, columns)
    bf16, f32 = jnp.bfloat16, jnp.float32
    dma = pltpu.SemaphoreType.DMA
    order = nf * rows
    moved = pltpu.VMEM((SLOTS, nf, rows, columns), bf16)
    flat = pltpu.VMEM((SLOTS * nf, rows, columns), bf16)
    square = pltpu.VMEM((SLOTS, order, columns), bf16)
    hbm = pl.BlockSpec(memory_space=pl.ANY)
    cut_scratch = []
    for (_, _, merged), width in zip(CUTS, column_cuts(columns)[1]):
        part = pltpu.VMEM((NY, nb, rows, width), bf16)
        group = pltpu.VMEM((nb, rows, width), bf16)
        per = SLOTS if merged else 1
        sent = pltpu.VMEM((SLOTS // per, nf, per, rows, width), bf16)
        cut_scratch += [part, part, group, group, group, group, sent, sent]
    vmem = pl.BlockSpec(memory_space=pltpu.VMEM)

    def stay(array):
        return pltpu.with_memory_space_constraint(array, pltpu.HBM)

    made = pl.pallas_call(
        functools.partial(kernel, nx, nz),
        out_shape=(
            pltpu.VMEM((nb, rows, columns), bf16),
            pltpu.VMEM((nb, rows, columns), f32),
            pltpu.VMEM((nb, rows, columns), bf16),
        ),
        in_specs=[hbm, hbm, hbm, hbm, hbm, hbm],
        out_specs=(vmem, vmem, vmem),
        scratch_shapes=cut_scratch + [
            pltpu.VMEM((16, 128), jnp.int32), pltpu.SMEM((nb,), jnp.int32), pltpu.SMEM((16, 128), jnp.int32),
            moved, flat, moved, moved, moved, flat,
            pltpu.VMEM((nb, rows, columns), bf16),
            pltpu.VMEM((nb, rows, columns), f32),
            square, square, square,
            pltpu.VMEM((SLOTS, order, columns), f32),
            square, square,
            dma((6,)), dma((NC, NY)), dma((NC, NY)), dma((NC, NY)), dma((NC, 6)), dma((NC, 6)),
            dma((NC, SLOTS)), dma((NC, SLOTS)),
            dma((SLOTS,)), dma((SLOTS,)), dma((SLOTS,)), dma((SLOTS,)), dma((SLOTS,)), dma((SLOTS,)),
            pltpu.SemaphoreType.REGULAR((4,)),
        ],
        compiler_params=pltpu.CompilerParams(
            collective_id=0, has_side_effects=True, vmem_limit_bytes=VMEM_BYTES
        ),
        cost_estimate=pl.CostEstimate(
            flops=SLOTS * 8 * order * columns * columns, bytes_accessed=16 * 1024 * 1024, transcendentals=0
        ),
    )(
        stay(owner_list.reshape(nb)), stay(grads), stay(first_moment), stay(second_moment),
        stay(left_basis.reshape(SLOTS, order, order)), stay(right_basis.reshape(SLOTS, columns, columns)),
    )
    return pl.pallas_call(
        deliver,
        out_shape=(
            jax.ShapeDtypeStruct((nb, rows, columns), bf16),
            jax.ShapeDtypeStruct((nb, rows, columns), f32),
            jax.ShapeDtypeStruct((nb, rows, columns), bf16),
        ),
        in_specs=[vmem, vmem, vmem],
        out_specs=(hbm, hbm, hbm),
        scratch_shapes=[dma((3,))],
        compiler_params=pltpu.CompilerParams(vmem_limit_bytes=DELIVER_VMEM_BYTES),
    )(*(pltpu.with_memory_space_constraint(array, pltpu.VMEM) for array in made))


def solution(mesh):
    nf = mesh.shape["fsdp"]
    nz = min(8, nf // 2)
    placed = (
        P("dp", None, "fsdp", None),
        P("dp", "fsdp", None),
        P("dp", "fsdp", None),
        P("dp", "fsdp", None, None, None),
        P("dp", "fsdp", None, None, None),
        P("dp", None, None),
    )
    return jax.shard_map(
        functools.partial(per_device, nf // nz, nz),
        mesh=mesh,
        in_specs=placed,
        out_specs=(P("dp", "fsdp", None), P("dp", "fsdp", None), P("dp", "fsdp", None)),
        check_vma=False,
    )
```

```python
import functools

import jax
import jax.numpy as jnp
from jax import lax
from jax.experimental import pallas as pl
from jax.experimental.pallas import tpu as pltpu
from jax.sharding import PartitionSpec as P

BETA_FIRST = 0.9
BETA_SECOND = 0.95
EPSILON = 1e-08

MESH = pl.DeviceIdType.MESH
VMEM_BYTES = 32 * 1024 * 1024
DELIVER_VMEM_BYTES = 8 * 1024 * 1024
NY = 4
SLOTS = 2
CUTS = ((2, False, True), (2, False, True), (2, False, True), (2, False, False))
NC = len(CUTS)


def column_cuts(columns):
    widths = [columns * eighths // 8 for eighths, _, _ in CUTS]
    return [sum(widths[:c]) for c in range(NC)], widths


def z_order(nz):
    order = [0]
    for step in range(1, nz // 2 + 1):
        order.append(step)
        if nz - step != step:
            order.append(nz - step)
    return order[::-1]


def adam(rotated, first, second):
    wide = rotated.astype(jnp.float32)
    first_wide = BETA_FIRST * first.astype(jnp.float32) + (1.0 - BETA_FIRST) * wide
    second_new = BETA_SECOND * second + (1.0 - BETA_SECOND) * wide * wide
    return first_wide, second_new


def kernel(
    nx, nz,
    owners, grads, first_hbm, second_hbm, left_hbm, right_hbm,
    first_new, second_new, update,
    *scratch,
):
    cut_refs = [scratch[c * 8:c * 8 + 8] for c in range(NC)]
    own, other, far, from_down, from_up, grad, g_send, g_recv = zip(*cut_refs)
    (
        stage, stage_sem, table, named_blocks, places,
        r_send, r_recv, d_send, d_recv, u_send, u_recv,
        first, second, left, right, left_t, total, half, back,
        load_sem, own_sem, pair_send, pair_recv, y_send, y_recv,
        g_ssem, g_rsem, r_ssem, r_rsem, d_ssem, d_rsem, u_ssem, u_rsem, round_sem,
    ) = scratch[NC * 8:]
    nf = nx * nz
    nb, rows, columns = first.shape
    starts, widths = column_cuts(columns)
    d, me = lax.axis_index("dp"), lax.axis_index("fsdp")
    y, core = d // 2, d % 2
    x, z = me // nz, me % nz
    up, down = (y + 1) % NY, (y + NY - 1) % NY
    at_up, at_down, at_pair = (up * 2 + core, me), (down * 2 + core, me), (y * 2 + 1 - core, me)
    at_far = (((y + 2) % NY) * 2 + core, me)
    order = z_order(nz)

    chips = [(y + 2) % NY, up, down, y]
    loads = [
        pltpu.make_async_copy(ref, to, load_sem.at[i])
        for i, (ref, to) in enumerate(
            [(left_hbm, left), (right_hbm, right), (first_hbm, first), (second_hbm, second)]
        )
    ]
    cols = [pl.ds(starts[c], widths[c]) for c in range(NC)]
    owns = [
        [
            pltpu.make_async_copy(grads.at[chips[r], core, :, :, cols[c]], own[c].at[r], own_sem.at[c, r])
            for r in range(NY)
        ]
        for c in range(NC)
    ]
    owner_load = pltpu.make_async_copy(owners, named_blocks, load_sem.at[5])
    owner_load.start()
    stages = [
        pltpu.make_async_copy(grads.at[chips[r], 1 - core, :, :, cols[0]], stage.at[r], stage_sem.at[r])
        for r in range(NY)
    ]
    for r in range(NY):
        stages[r].start()
        owns[0][r].start()

    def find_places():
        owner_load.wait()
        lane = lax.broadcasted_iota(jnp.int32, (8, 128), 1)
        zero = jnp.zeros((8, 128), jnp.int32)

        def step(j, carry):
            count, source, named = carry
            owner = named_blocks[j]
            match = lane % nf == owner
            source = jnp.where(jnp.logical_and(match, count == lane // nf), j, source)
            return count + match.astype(jnp.int32), source, jnp.where(lane == j, owner, named)

        _, source, named = lax.fori_loop(0, nb, step, (zero, zero, zero))

        def earlier(i, slot):
            return slot + jnp.logical_and(named == named_blocks[i], lane > i).astype(jnp.int32)

        table[0:8] = source
        table[8:16] = jnp.minimum(lax.fori_loop(0, nb, earlier, zero), SLOTS - 1) * nf + named
        copy = pltpu.make_async_copy(table, places, load_sem.at[4])
        copy.start()
        copy.wait()

    barrier = pltpu.get_barrier_semaphore()

    def across(dx, dz):
        return d, ((x + nx + dx) % nx) * nz + (z + nz + dz) % nz

    near = [at_pair, at_far, at_up, at_down, across(0, 1), across(0, -1), across(1, 0), across(-1, 0)]
    for device in near:
        pl.semaphore_signal(barrier, inc=1, device_id=device, device_id_type=MESH)
    pl.semaphore_wait(barrier, len(near))

    rounds = [[(0, 1), (0, -1)], [(0, 2), (0, -2)]] if nz > 2 else []
    rounds.append([(1, 0), (-1, 0)])
    if nx > 2:
        rounds.append([(2, 0)])

    def tell(k):
        for dx, dz in rounds[k]:
            pl.semaphore_signal(round_sem.at[k], inc=1, device_id=across(dx, dz), device_id_type=MESH)

    def hear(k):
        if k < len(rounds):
            pl.semaphore_wait(round_sem.at[k], len(rounds[k]))
            if k + 1 < len(rounds):
                tell(k + 1)

    tell(0)

    def remote(source, target, send, recv, device):
        return pltpu.make_async_remote_copy(
            src_ref=source, dst_ref=target, send_sem=send, recv_sem=recv, device_id=device, device_id_type=MESH
        )

    pairs = [
        [
            remote(
                stage.at[r] if c == 0 else grads.at[chips[r], 1 - core, :, :, cols[c]], other[c].at[r],
                pair_send.at[c, r], pair_recv.at[c, r], at_pair,
            )
            for r in range(NY)
        ]
        for c in range(NC)
    ]
    for c in range(NC):
        for r in range(NY):
            if c == 0:
                stages[r].wait()
            pairs[c][r].start()
            if c > 0:
                owns[c][r].start()
    for load in loads:
        load.start()

    low, high = pl.ds(0, nb // 2), pl.ds(nb // 2, nb // 2)

    def y_hop(c, i, source, target, device):
        return remote(source, target, y_send.at[c, i], y_recv.at[c, i], device)

    hops = [
        [
            y_hop(c, 0, own[c].at[0], far[c], at_far),
            y_hop(c, 1, own[c].at[1], from_down[c], at_up),
            y_hop(c, 2, own[c].at[2], from_up[c], at_down),
        ]
        if CUTS[c][1]
        else [
            y_hop(c, 0, own[c].at[0, low], far[c].at[low], at_up),
            y_hop(c, 1, own[c].at[0, high], far[c].at[high], at_down),
            y_hop(c, 2, own[c].at[1, high], from_down[c].at[high], at_up),
            y_hop(c, 3, own[c].at[2, low], from_up[c].at[low], at_down),
            y_hop(c, 4, own[c].at[1, low], from_down[c].at[low], at_up),
            y_hop(c, 5, own[c].at[2, high], from_up[c].at[high], at_down),
        ]
        for c in range(NC)
    ]
    group = min(4, nb // 2)

    def wide(ref, *at):
        return ref[at].astype(jnp.float32)

    def pair_sum(c, r):
        owns[c][r].wait()
        pairs[c][r].wait_recv()

        def step(j, carry):
            blocks = pl.ds(j * group, group)
            own[c][r, blocks] = (wide(own[c], r, blocks) + wide(other[c], r, blocks)).astype(jnp.bfloat16)
            return carry

        lax.fori_loop(0, nb // group, step, 0)

    def add_far(c, r, first_block):
        def step(j, carry):
            blocks = pl.ds(first_block + j * group, group)
            own[c][r, blocks] = (wide(own[c], r, blocks) + wide(far[c], blocks)).astype(jnp.bfloat16)
            return carry

        lax.fori_loop(0, nb // 2 // group, step, 0)

    def spread(c):
        pair_sum(c, 0)
        hops[c][0].start()
        if not CUTS[c][1]:
            hops[c][1].start()
        pair_sum(c, 1)
        hops[c][1 if CUTS[c][1] else 2].start()
        pair_sum(c, 2)
        hops[c][2 if CUTS[c][1] else 3].start()

    def forward(c):
        if CUTS[c][1]:
            return
        hops[c][0].wait_recv()
        add_far(c, 1, 0)
        hops[c][4].start()
        hops[c][1].wait_recv()
        add_far(c, 2, nb // 2)
        hops[c][5].start()

    def finish(c):
        pair_sum(c, 3)
        straight = CUTS[c][1]
        for hop in hops[c][0 if straight else 2:]:
            hop.wait_recv()

        def step(j, carry):
            blocks = pl.ds(j * group, group)
            summed = wide(own[c], 3, blocks) + wide(from_down[c], blocks) + wide(from_up[c], blocks)
            if straight:
                summed = summed + wide(far[c], blocks)
            grad[c][blocks] = summed.astype(jnp.bfloat16)
            return carry

        lax.fori_loop(0, nb // group, step, 0)

    def exchange(send, recv, at, ssem, rsem, fill_plane=None, fill=None, flat=False):
        mine = (at[0] * nf + me,) if flat else (*at, me)

        def plane(i, carry):
            px = (x + nx // 2 + i) % nx
            if fill_plane is not None:
                fill_plane(px)
            for dz in order:
                p = px * nz + (z + dz) % nz
                if fill is not None:
                    fill(p)
                source, target = send.at[(*at, p)], recv.at[mine]
                if dz == 0:
                    @pl.when(i != nx - nx // 2)
                    def _():
                        remote(source, target, ssem, rsem, (d, p)).start()

                    @pl.when(i == nx - nx // 2)
                    def _():
                        recv[mine] = send[(*at, me)]
                else:
                    remote(source, target, ssem, rsem, (d, p)).start()
            return carry

        lax.fori_loop(0, nx, plane, 0)

    def arrived(ref, at, rsem, flat=False):
        whole = ref.at[pl.ds(at[0] * nf, nf - 1)] if flat else ref.at[(*at, pl.ds(0, nf - 1))]
        pltpu.make_async_copy(whole, whole, rsem).wait()

    def send_grad(c, stream):
        per = SLOTS if CUTS[c][2] else 1

        def fill(p):
            for i in range(per):
                g_send[c][stream, p, i] = grad[c][places[0, (stream * per + i) * nf + p]]

        exchange(g_send[c], g_recv[c], (stream,), g_ssem.at[c, stream], g_rsem.at[c, stream], fill=fill)

    streams = [range(1) if CUTS[c][2] else range(SLOTS) for c in range(NC)]
    span = nz * rows

    def product(c, s, t):
        at = (0, pl.ds(t * nz, nz), s) if CUTS[c][2] else (s, pl.ds(t * nz, nz), 0)
        held = g_recv[c][at].reshape(span, widths[c])
        return jnp.dot(held, right[s, cols[c], :], preferred_element_type=jnp.float32)

    def add_products(c, s):
        def step(t, carry):
            piece = pl.ds(t * span, span)
            made = product(c, s, t)
            if c > 0:
                made = total[s, piece] + made
            if c < NC - 1:
                total[s, piece] = made
            else:
                half[s, piece] = made.astype(jnp.bfloat16)
            return carry

        lax.fori_loop(0, nx, step, 0)

    hear(0)
    spread(0)
    for c in range(1, NC):
        if c == 1:
            hear(1)
            find_places()
            hear(2)
        forward(c - 1)
        if c == 1:
            hear(3)
        spread(c)
        finish(c - 1)
        for stream in streams[c - 1]:
            send_grad(c - 1, stream)
    forward(NC - 1)
    finish(NC - 1)
    for stream in streams[NC - 1]:
        send_grad(NC - 1, stream)

    for load in loads:
        load.wait()
    for s in range(SLOTS):
        for t in range(nx):
            piece = pl.ds(t * nz * rows, nz * rows)
            left_t[s, :, piece] = left[s, piece, :].T

    for c in range(NC - 1):
        for stream in streams[c]:
            arrived(g_recv[c], (stream,), g_rsem.at[c, stream])
        for s in range(SLOTS):
            add_products(c, s)

    for s in range(SLOTS):
        if s < len(streams[NC - 1]):
            arrived(g_recv[NC - 1], (s,), g_rsem.at[NC - 1, s])
        add_products(NC - 1, s)

        def rotate(px, s=s):
            made = jnp.dot(left_t[s, pl.ds(px * span, span)], half[s], preferred_element_type=jnp.float32)
            r_send[s, pl.ds(px * nz, nz)] = made.astype(jnp.bfloat16).reshape(nz, rows, columns)

        exchange(r_send, r_recv, (s,), r_ssem.at[s], r_rsem.at[s], fill_plane=rotate, flat=True)

    for s in range(SLOTS):
        arrived(r_recv, (s,), r_rsem.at[s], flat=True)

        def direct(p, s=s):
            block = places[0, s * nf + p]
            first_wide, second_wide = adam(r_recv[s * nf + p], first[block], second[block])
            d_send[s, p] = (first_wide / (jnp.sqrt(second_wide) + EPSILON)).astype(jnp.bfloat16)

        exchange(d_send, d_recv, (s,), d_ssem.at[s], d_rsem.at[s], fill=direct)

    def moments(j, carry):
        first_wide, second_wide = adam(r_recv[places[8, j]], first[j], second[j])
        first_new[j] = first_wide.astype(jnp.bfloat16)
        second_new[j] = second_wide
        return carry

    lax.fori_loop(0, nb, moments, 0)
    for s in range(SLOTS):
        arrived(d_recv, (s,), d_rsem.at[s])

        def undo_right(t, carry, s=s):
            held = d_recv[s, pl.ds(t * nz, nz)].reshape(span, columns)
            made = lax.dot_general(held, right[s], (((1,), (1,)), ((), ())), preferred_element_type=jnp.float32)
            back[s, pl.ds(t * span, span)] = made.astype(jnp.bfloat16)
            return carry

        lax.fori_loop(0, nx, undo_right, 0)

        def undo_left(px, s=s):
            made = jnp.dot(left[s, pl.ds(px * span, span)], back[s], preferred_element_type=jnp.float32)
            u_send[s, pl.ds(px * nz, nz)] = made.astype(jnp.bfloat16).reshape(nz, rows, columns)

        exchange(u_send, u_recv, (s,), u_ssem.at[s], u_rsem.at[s], fill_plane=undo_left, flat=True)

    for c in range(NC):
        for r in range(NY):
            pairs[c][r].wait_send()
        for hop in hops[c]:
            hop.wait_send()
        for s in streams[c]:
            arrived(g_send[c], (s,), g_ssem.at[c, s])
    for s in range(SLOTS):
        arrived(r_send, (s,), r_ssem.at[s])
        arrived(d_send, (s,), d_ssem.at[s])
        arrived(u_send, (s,), u_ssem.at[s])

    for s in range(SLOTS):
        arrived(u_recv, (s,), u_rsem.at[s], flat=True)

    def pick(j, carry):
        update[j] = u_recv[places[8, j]]
        return carry

    lax.fori_loop(0, nb, pick, 0)


def deliver(*refs):
    count = (len(refs) - 1) // 2
    copies = [pltpu.make_async_copy(refs[i], refs[count + i], refs[-1].at[i]) for i in range(count)]
    for copy in copies:
        copy.start()
    for copy in copies:
        copy.wait()


def per_device(nx, nz, grad_parts, first_moment, second_moment, left_basis, right_basis, owner_list):
    nf = nx * nz
    nb, rows, columns = first_moment.shape
    grads = grad_parts.reshape(NY, 2, nb, rows, columns)
    bf16, f32 = jnp.bfloat16, jnp.float32
    dma = pltpu.SemaphoreType.DMA
    order = nf * rows
    moved = pltpu.VMEM((SLOTS, nf, rows, columns), bf16)
    flat = pltpu.VMEM((SLOTS * nf, rows, columns), bf16)
    square = pltpu.VMEM((SLOTS, order, columns), bf16)
    hbm = pl.BlockSpec(memory_space=pl.ANY)
    cut_scratch = []
    for (_, _, merged), width in zip(CUTS, column_cuts(columns)[1]):
        part = pltpu.VMEM((NY, nb, rows, width), bf16)
        group = pltpu.VMEM((nb, rows, width), bf16)
        per = SLOTS if merged else 1
        sent = pltpu.VMEM((SLOTS // per, nf, per, rows, width), bf16)
        cut_scratch += [part, part, group, group, group, group, sent, sent]
    vmem = pl.BlockSpec(memory_space=pltpu.VMEM)

    def stay(array):
        return pltpu.with_memory_space_constraint(array, pltpu.HBM)

    made = pl.pallas_call(
        functools.partial(kernel, nx, nz),
        out_shape=(
            pltpu.VMEM((nb, rows, columns), bf16),
            pltpu.VMEM((nb, rows, columns), f32),
            pltpu.VMEM((nb, rows, columns), bf16),
        ),
        in_specs=[hbm, hbm, hbm, hbm, hbm, hbm],
        out_specs=(vmem, vmem, vmem),
        scratch_shapes=cut_scratch + [
            pltpu.VMEM((NY, nb, rows, column_cuts(columns)[1][0]), bf16), dma((NY,)),
            pltpu.VMEM((16, 128), jnp.int32), pltpu.SMEM((nb,), jnp.int32), pltpu.SMEM((16, 128), jnp.int32),
            moved, flat, moved, moved, moved, flat,
            pltpu.VMEM((nb, rows, columns), bf16),
            pltpu.VMEM((nb, rows, columns), f32),
            square, square, square,
            pltpu.VMEM((SLOTS, order, columns), f32),
            square, square,
            dma((6,)), dma((NC, NY)), dma((NC, NY)), dma((NC, NY)), dma((NC, 6)), dma((NC, 6)),
            dma((NC, SLOTS)), dma((NC, SLOTS)),
            dma((SLOTS,)), dma((SLOTS,)), dma((SLOTS,)), dma((SLOTS,)), dma((SLOTS,)), dma((SLOTS,)),
            pltpu.SemaphoreType.REGULAR((4,)),
        ],
        compiler_params=pltpu.CompilerParams(
            collective_id=0, has_side_effects=True, vmem_limit_bytes=VMEM_BYTES
        ),
        cost_estimate=pl.CostEstimate(
            flops=SLOTS * 8 * order * columns * columns, bytes_accessed=16 * 1024 * 1024, transcendentals=0
        ),
    )(
        stay(owner_list.reshape(nb)), stay(grads), stay(first_moment), stay(second_moment),
        stay(left_basis.reshape(SLOTS, order, order)), stay(right_basis.reshape(SLOTS, columns, columns)),
    )
    return pl.pallas_call(
        deliver,
        out_shape=(
            jax.ShapeDtypeStruct((nb, rows, columns), bf16),
            jax.ShapeDtypeStruct((nb, rows, columns), f32),
            jax.ShapeDtypeStruct((nb, rows, columns), bf16),
        ),
        in_specs=[vmem, vmem, vmem],
        out_specs=(hbm, hbm, hbm),
        scratch_shapes=[dma((3,))],
        compiler_params=pltpu.CompilerParams(vmem_limit_bytes=DELIVER_VMEM_BYTES),
    )(*(pltpu.with_memory_space_constraint(array, pltpu.VMEM) for array in made))


def solution(mesh):
    nf = mesh.shape["fsdp"]
    nz = min(8, nf // 2)
    placed = (
        P("dp", None, "fsdp", None),
        P("dp", "fsdp", None),
        P("dp", "fsdp", None),
        P("dp", "fsdp", None, None, None),
        P("dp", "fsdp", None, None, None),
        P("dp", None, None),
    )
    return jax.shard_map(
        functools.partial(per_device, nf // nz, nz),
        mesh=mesh,
        in_specs=placed,
        out_specs=(P("dp", "fsdp", None), P("dp", "fsdp", None), P("dp", "fsdp", None)),
        check_vma=False,
    )
```

```python
import functools

import jax
import jax.numpy as jnp
from jax import lax
from jax.experimental import pallas as pl
from jax.experimental.pallas import tpu as pltpu
from jax.sharding import PartitionSpec as P

BETA_FIRST = 0.9
BETA_SECOND = 0.95
EPSILON = 1e-08

MESH = pl.DeviceIdType.MESH
VMEM_BYTES = 32 * 1024 * 1024
DELIVER_VMEM_BYTES = 8 * 1024 * 1024
NY = 4
SLOTS = 2
CUTS = ((2, False, True), (2, False, True), (2, False, True), (2, False, False))
NC = len(CUTS)


def column_cuts(columns):
    widths = [columns * eighths // 8 for eighths, _, _ in CUTS]
    return [sum(widths[:c]) for c in range(NC)], widths


def z_order(nz):
    order = [0]
    for step in range(1, nz // 2 + 1):
        order.append(step)
        if nz - step != step:
            order.append(nz - step)
    return order[::-1]


def adam(rotated, first, second):
    wide = rotated.astype(jnp.float32)
    first_wide = BETA_FIRST * first.astype(jnp.float32) + (1.0 - BETA_FIRST) * wide
    second_new = BETA_SECOND * second + (1.0 - BETA_SECOND) * wide * wide
    return first_wide, second_new


def kernel(
    nx, nz,
    owners, grads, first_hbm, second_hbm, left_hbm, right_hbm,
    first_new, second_new, update,
    *scratch,
):
    cut_refs = [scratch[c * 8:c * 8 + 8] for c in range(NC)]
    own, other, far, from_down, from_up, grad, g_send, g_recv = zip(*cut_refs)
    (
        stage, stage_sem, table, named_blocks, places,
        r_send, r_recv, d_send, d_recv, u_send, u_recv,
        first, second, left, right, left_t, total, half, back,
        load_sem, own_sem, pair_send, pair_recv, y_send, y_recv,
        g_ssem, g_rsem, r_ssem, r_rsem, d_ssem, d_rsem, u_ssem, u_rsem, round_sem,
    ) = scratch[NC * 8:]
    nf = nx * nz
    nb, rows, columns = first.shape
    starts, widths = column_cuts(columns)
    d, me = lax.axis_index("dp"), lax.axis_index("fsdp")
    y, core = d // 2, d % 2
    x, z = me // nz, me % nz
    up, down = (y + 1) % NY, (y + NY - 1) % NY
    at_up, at_down, at_pair = (up * 2 + core, me), (down * 2 + core, me), (y * 2 + 1 - core, me)
    at_far = (((y + 2) % NY) * 2 + core, me)
    order = z_order(nz)

    chips = [(y + 2) % NY, up, down, y]
    loads = [
        pltpu.make_async_copy(ref, to, load_sem.at[i])
        for i, (ref, to) in enumerate(
            [(left_hbm, left), (right_hbm, right), (first_hbm, first), (second_hbm, second)]
        )
    ]
    cols = [pl.ds(starts[c], widths[c]) for c in range(NC)]
    owns = [
        [
            pltpu.make_async_copy(grads.at[chips[r], core, :, :, cols[c]], own[c].at[r], own_sem.at[c, r])
            for r in range(NY)
        ]
        for c in range(NC)
    ]
    owner_load = pltpu.make_async_copy(owners, named_blocks, load_sem.at[5])
    owner_load.start()
    stages = [
        pltpu.make_async_copy(grads.at[chips[r], 1 - core, :, :, cols[0]], stage.at[r], stage_sem.at[r])
        for r in range(NY)
    ]
    for r in range(NY):
        stages[r].start()
        owns[0][r].start()

    def find_places():
        owner_load.wait()
        lane = lax.broadcasted_iota(jnp.int32, (8, 128), 1)
        zero = jnp.zeros((8, 128), jnp.int32)

        def step(j, carry):
            count, source, named = carry
            owner = named_blocks[j]
            match = lane % nf == owner
            source = jnp.where(jnp.logical_and(match, count == lane // nf), j, source)
            return count + match.astype(jnp.int32), source, jnp.where(lane == j, owner, named)

        _, source, named = lax.fori_loop(0, nb, step, (zero, zero, zero))

        def earlier(i, slot):
            return slot + jnp.logical_and(named == named_blocks[i], lane > i).astype(jnp.int32)

        table[0:8] = source
        table[8:16] = jnp.minimum(lax.fori_loop(0, nb, earlier, zero), SLOTS - 1) * nf + named
        copy = pltpu.make_async_copy(table, places, load_sem.at[4])
        copy.start()
        copy.wait()

    barrier = pltpu.get_barrier_semaphore()

    def across(dx, dz):
        return d, ((x + nx + dx) % nx) * nz + (z + nz + dz) % nz

    near = [at_pair, at_far, at_up, at_down, across(0, 1), across(0, -1), across(1, 0), across(-1, 0)]
    for device in near:
        pl.semaphore_signal(barrier, inc=1, device_id=device, device_id_type=MESH)
    pl.semaphore_wait(barrier, len(near))

    rounds = [[(0, 1), (0, -1)], [(0, 2), (0, -2)]] if nz > 2 else []
    rounds.append([(1, 0), (-1, 0)])
    if nx > 2:
        rounds.append([(2, 0)])

    def tell(k):
        for dx, dz in rounds[k]:
            pl.semaphore_signal(round_sem.at[k], inc=1, device_id=across(dx, dz), device_id_type=MESH)

    def hear(k):
        if k < len(rounds):
            pl.semaphore_wait(round_sem.at[k], len(rounds[k]))
            if k + 1 < len(rounds):
                tell(k + 1)

    tell(0)

    def remote(source, target, send, recv, device):
        return pltpu.make_async_remote_copy(
            src_ref=source, dst_ref=target, send_sem=send, recv_sem=recv, device_id=device, device_id_type=MESH
        )

    pairs = [
        [
            remote(
                stage.at[r] if c == 0 else grads.at[chips[r], 1 - core, :, :, cols[c]], other[c].at[r],
                pair_send.at[c, r], pair_recv.at[c, r], at_pair,
            )
            for r in range(NY)
        ]
        for c in range(NC)
    ]
    for r in range(NY):
        stages[r].wait()
        pairs[0][r].start()

    low, high = pl.ds(0, nb // 2), pl.ds(nb // 2, nb // 2)

    def y_hop(c, i, source, target, device):
        return remote(source, target, y_send.at[c, i], y_recv.at[c, i], device)

    hops = [
        [
            y_hop(c, 0, own[c].at[0], far[c], at_far),
            y_hop(c, 1, own[c].at[1], from_down[c], at_up),
            y_hop(c, 2, own[c].at[2], from_up[c], at_down),
        ]
        if CUTS[c][1]
        else [
            y_hop(c, 0, own[c].at[0, low], far[c].at[low], at_up),
            y_hop(c, 1, own[c].at[0, high], far[c].at[high], at_down),
            y_hop(c, 2, own[c].at[1, high], from_down[c].at[high], at_up),
            y_hop(c, 3, own[c].at[2, low], from_up[c].at[low], at_down),
            y_hop(c, 4, own[c].at[1, low], from_down[c].at[low], at_up),
            y_hop(c, 5, own[c].at[2, high], from_up[c].at[high], at_down),
        ]
        for c in range(NC)
    ]
    group = min(4, nb // 2)

    def wide(ref, *at):
        return ref[at].astype(jnp.float32)

    def pair_sum(c, r):
        owns[c][r].wait()
        pairs[c][r].wait_recv()

        def step(j, carry):
            blocks = pl.ds(j * group, group)
            own[c][r, blocks] = (wide(own[c], r, blocks) + wide(other[c], r, blocks)).astype(jnp.bfloat16)
            return carry

        lax.fori_loop(0, nb // group, step, 0)

    def add_far(c, r, first_block):
        def step(j, carry):
            blocks = pl.ds(first_block + j * group, group)
            own[c][r, blocks] = (wide(own[c], r, blocks) + wide(far[c], blocks)).astype(jnp.bfloat16)
            return carry

        lax.fori_loop(0, nb // 2 // group, step, 0)

    def spread(c):
        pair_sum(c, 0)
        hops[c][0].start()
        if not CUTS[c][1]:
            hops[c][1].start()
        pair_sum(c, 1)
        hops[c][1 if CUTS[c][1] else 2].start()
        pair_sum(c, 2)
        hops[c][2 if CUTS[c][1] else 3].start()

    def forward(c):
        if CUTS[c][1]:
            return
        hops[c][0].wait_recv()
        add_far(c, 1, 0)
        hops[c][4].start()
        hops[c][1].wait_recv()
        add_far(c, 2, nb // 2)
        hops[c][5].start()

    def finish(c):
        pair_sum(c, 3)
        straight = CUTS[c][1]
        for hop in hops[c][0 if straight else 2:]:
            hop.wait_recv()

        def step(j, carry):
            blocks = pl.ds(j * group, group)
            summed = wide(own[c], 3, blocks) + wide(from_down[c], blocks) + wide(from_up[c], blocks)
            if straight:
                summed = summed + wide(far[c], blocks)
            grad[c][blocks] = summed.astype(jnp.bfloat16)
            return carry

        lax.fori_loop(0, nb // group, step, 0)

    def exchange(send, recv, at, ssem, rsem, fill_plane=None, fill=None, flat=False):
        mine = (at[0] * nf + me,) if flat else (*at, me)

        def plane(i, carry):
            px = (x + nx // 2 + i) % nx
            if fill_plane is not None:
                fill_plane(px)
            for dz in order:
                p = px * nz + (z + dz) % nz
                if fill is not None:
                    fill(p)
                source, target = send.at[(*at, p)], recv.at[mine]
                if dz == 0:
                    @pl.when(i != nx - nx // 2)
                    def _():
                        remote(source, target, ssem, rsem, (d, p)).start()

                    @pl.when(i == nx - nx // 2)
                    def _():
                        recv[mine] = send[(*at, me)]
                else:
                    remote(source, target, ssem, rsem, (d, p)).start()
            return carry

        lax.fori_loop(0, nx, plane, 0)

    def arrived(ref, at, rsem, flat=False):
        whole = ref.at[pl.ds(at[0] * nf, nf - 1)] if flat else ref.at[(*at, pl.ds(0, nf - 1))]
        pltpu.make_async_copy(whole, whole, rsem).wait()

    def send_grad(c, stream):
        per = SLOTS if CUTS[c][2] else 1

        def fill(p):
            for i in range(per):
                g_send[c][stream, p, i] = grad[c][places[0, (stream * per + i) * nf + p]]

        exchange(g_send[c], g_recv[c], (stream,), g_ssem.at[c, stream], g_rsem.at[c, stream], fill=fill)

    streams = [range(1) if CUTS[c][2] else range(SLOTS) for c in range(NC)]
    span = nz * rows

    def product(c, s, t):
        at = (0, pl.ds(t * nz, nz), s) if CUTS[c][2] else (s, pl.ds(t * nz, nz), 0)
        held = g_recv[c][at].reshape(span, widths[c])
        return jnp.dot(held, right[s, cols[c], :], preferred_element_type=jnp.float32)

    def add_products(c, s):
        def step(t, carry):
            piece = pl.ds(t * span, span)
            made = product(c, s, t)
            if c > 0:
                made = total[s, piece] + made
            if c < NC - 1:
                total[s, piece] = made
            else:
                half[s, piece] = made.astype(jnp.bfloat16)
            return carry

        lax.fori_loop(0, nx, step, 0)

    hear(0)
    spread(0)
    for c in range(1, NC):
        if c == 1:
            for later in range(1, NC):
                for r in range(NY):
                    pairs[later][r].start()
                    owns[later][r].start()
            for load in loads:
                load.start()
            hear(1)
            find_places()
            hear(2)
        forward(c - 1)
        if c == 1:
            hear(3)
        spread(c)
        finish(c - 1)
        for stream in streams[c - 1]:
            send_grad(c - 1, stream)
    forward(NC - 1)
    finish(NC - 1)
    for stream in streams[NC - 1]:
        send_grad(NC - 1, stream)

    for load in loads:
        load.wait()
    for s in range(SLOTS):
        for t in range(nx):
            piece = pl.ds(t * nz * rows, nz * rows)
            left_t[s, :, piece] = left[s, piece, :].T

    for c in range(NC - 1):
        for stream in streams[c]:
            arrived(g_recv[c], (stream,), g_rsem.at[c, stream])
        for s in range(SLOTS):
            add_products(c, s)

    for s in range(SLOTS):
        if s < len(streams[NC - 1]):
            arrived(g_recv[NC - 1], (s,), g_rsem.at[NC - 1, s])
        add_products(NC - 1, s)

        def rotate(px, s=s):
            made = jnp.dot(left_t[s, pl.ds(px * span, span)], half[s], preferred_element_type=jnp.float32)
            r_send[s, pl.ds(px * nz, nz)] = made.astype(jnp.bfloat16).reshape(nz, rows, columns)

        exchange(r_send, r_recv, (s,), r_ssem.at[s], r_rsem.at[s], fill_plane=rotate, flat=True)

    for s in range(SLOTS):
        arrived(r_recv, (s,), r_rsem.at[s], flat=True)

        def direct(p, s=s):
            block = places[0, s * nf + p]
            first_wide, second_wide = adam(r_recv[s * nf + p], first[block], second[block])
            d_send[s, p] = (first_wide / (jnp.sqrt(second_wide) + EPSILON)).astype(jnp.bfloat16)

        exchange(d_send, d_recv, (s,), d_ssem.at[s], d_rsem.at[s], fill=direct)

    def moments(j, carry):
        first_wide, second_wide = adam(r_recv[places[8, j]], first[j], second[j])
        first_new[j] = first_wide.astype(jnp.bfloat16)
        second_new[j] = second_wide
        return carry

    lax.fori_loop(0, nb, moments, 0)
    for s in range(SLOTS):
        arrived(d_recv, (s,), d_rsem.at[s])

        def undo_right(t, carry, s=s):
            held = d_recv[s, pl.ds(t * nz, nz)].reshape(span, columns)
            made = lax.dot_general(held, right[s], (((1,), (1,)), ((), ())), preferred_element_type=jnp.float32)
            back[s, pl.ds(t * span, span)] = made.astype(jnp.bfloat16)
            return carry

        lax.fori_loop(0, nx, undo_right, 0)

        def undo_left(px, s=s):
            made = jnp.dot(left[s, pl.ds(px * span, span)], back[s], preferred_element_type=jnp.float32)
            u_send[s, pl.ds(px * nz, nz)] = made.astype(jnp.bfloat16).reshape(nz, rows, columns)

        exchange(u_send, u_recv, (s,), u_ssem.at[s], u_rsem.at[s], fill_plane=undo_left, flat=True)

    for c in range(NC):
        for r in range(NY):
            pairs[c][r].wait_send()
        for hop in hops[c]:
            hop.wait_send()
        for s in streams[c]:
            arrived(g_send[c], (s,), g_ssem.at[c, s])
    for s in range(SLOTS):
        arrived(r_send, (s,), r_ssem.at[s])
        arrived(d_send, (s,), d_ssem.at[s])
        arrived(u_send, (s,), u_ssem.at[s])

    for s in range(SLOTS):
        arrived(u_recv, (s,), u_rsem.at[s], flat=True)

    def pick(j, carry):
        update[j] = u_recv[places[8, j]]
        return carry

    lax.fori_loop(0, nb, pick, 0)


def deliver(*refs):
    count = (len(refs) - 1) // 2
    copies = [pltpu.make_async_copy(refs[i], refs[count + i], refs[-1].at[i]) for i in range(count)]
    for copy in copies:
        copy.start()
    for copy in copies:
        copy.wait()


def per_device(nx, nz, grad_parts, first_moment, second_moment, left_basis, right_basis, owner_list):
    nf = nx * nz
    nb, rows, columns = first_moment.shape
    grads = grad_parts.reshape(NY, 2, nb, rows, columns)
    bf16, f32 = jnp.bfloat16, jnp.float32
    dma = pltpu.SemaphoreType.DMA
    order = nf * rows
    moved = pltpu.VMEM((SLOTS, nf, rows, columns), bf16)
    flat = pltpu.VMEM((SLOTS * nf, rows, columns), bf16)
    square = pltpu.VMEM((SLOTS, order, columns), bf16)
    hbm = pl.BlockSpec(memory_space=pl.ANY)
    cut_scratch = []
    for (_, _, merged), width in zip(CUTS, column_cuts(columns)[1]):
        part = pltpu.VMEM((NY, nb, rows, width), bf16)
        group = pltpu.VMEM((nb, rows, width), bf16)
        per = SLOTS if merged else 1
        sent = pltpu.VMEM((SLOTS // per, nf, per, rows, width), bf16)
        cut_scratch += [part, part, group, group, group, group, sent, sent]
    vmem = pl.BlockSpec(memory_space=pltpu.VMEM)

    def stay(array):
        return pltpu.with_memory_space_constraint(array, pltpu.HBM)

    made = pl.pallas_call(
        functools.partial(kernel, nx, nz),
        out_shape=(
            pltpu.VMEM((nb, rows, columns), bf16),
            pltpu.VMEM((nb, rows, columns), f32),
            pltpu.VMEM((nb, rows, columns), bf16),
        ),
        in_specs=[hbm, hbm, hbm, hbm, hbm, hbm],
        out_specs=(vmem, vmem, vmem),
        scratch_shapes=cut_scratch + [
            pltpu.VMEM((NY, nb, rows, column_cuts(columns)[1][0]), bf16), dma((NY,)),
            pltpu.VMEM((16, 128), jnp.int32), pltpu.SMEM((nb,), jnp.int32), pltpu.SMEM((16, 128), jnp.int32),
            moved, flat, moved, moved, moved, flat,
            pltpu.VMEM((nb, rows, columns), bf16),
            pltpu.VMEM((nb, rows, columns), f32),
            square, square, square,
            pltpu.VMEM((SLOTS, order, columns), f32),
            square, square,
            dma((6,)), dma((NC, NY)), dma((NC, NY)), dma((NC, NY)), dma((NC, 6)), dma((NC, 6)),
            dma((NC, SLOTS)), dma((NC, SLOTS)),
            dma((SLOTS,)), dma((SLOTS,)), dma((SLOTS,)), dma((SLOTS,)), dma((SLOTS,)), dma((SLOTS,)),
            pltpu.SemaphoreType.REGULAR((4,)),
        ],
        compiler_params=pltpu.CompilerParams(
            collective_id=0, has_side_effects=True, vmem_limit_bytes=VMEM_BYTES
        ),
        cost_estimate=pl.CostEstimate(
            flops=SLOTS * 8 * order * columns * columns, bytes_accessed=16 * 1024 * 1024, transcendentals=0
        ),
    )(
        stay(owner_list.reshape(nb)), stay(grads), stay(first_moment), stay(second_moment),
        stay(left_basis.reshape(SLOTS, order, order)), stay(right_basis.reshape(SLOTS, columns, columns)),
    )
    return pl.pallas_call(
        deliver,
        out_shape=(
            jax.ShapeDtypeStruct((nb, rows, columns), bf16),
            jax.ShapeDtypeStruct((nb, rows, columns), f32),
            jax.ShapeDtypeStruct((nb, rows, columns), bf16),
        ),
        in_specs=[vmem, vmem, vmem],
        out_specs=(hbm, hbm, hbm),
        scratch_shapes=[dma((3,))],
        compiler_params=pltpu.CompilerParams(vmem_limit_bytes=DELIVER_VMEM_BYTES),
    )(*(pltpu.with_memory_space_constraint(array, pltpu.VMEM) for array in made))


def solution(mesh):
    nf = mesh.shape["fsdp"]
    nz = min(8, nf // 2)
    placed = (
        P("dp", None, "fsdp", None),
        P("dp", "fsdp", None),
        P("dp", "fsdp", None),
        P("dp", "fsdp", None, None, None),
        P("dp", "fsdp", None, None, None),
        P("dp", None, None),
    )
    return jax.shard_map(
        functools.partial(per_device, nf // nz, nz),
        mesh=mesh,
        in_specs=placed,
        out_specs=(P("dp", "fsdp", None), P("dp", "fsdp", None), P("dp", "fsdp", None)),
        check_vma=False,
    )
```
